512 devices in a mesh: seq: 16 (over z, core), batch: 32 (over x, y).
Axes of the slice: x: 4, y: 8, z: 8, core: 2. Of those that a mesh axis runs over, the one named last changes fastest.
Arguments:
- queries: bfloat16 [65536, 4096], P(('batch', 'seq')), parts along dimension 0, may hold values from -12 to 12
- key_vectors: bfloat16 [65536, 4096], P(('batch', 'seq')), parts along dimension 0, may hold values from -12 to 12
- value_vectors: bfloat16 [65536, 4096], P(('batch', 'seq')), parts along dimension 0, may hold values from -6 to 6
- keep_list: int32 [1024, 96], P(('batch', 'seq')), parts along dimension 0, may hold values from 0 to 254, as said below
- block_counts: int32 [1024], P('batch'), parts along dimension 0, may hold values from 1 to 96, as said below
Outputs:
- attended: bfloat16 [65536, 4096], P(('batch', 'seq')), parts along dimension 0
The draws below stay inside these ranges and needn't reach their ends.
There are 32 independent parts, one for each index of `batch`. The reference program is written for one: setup_inputs(seed, part) draws one part's arguments, and reference() takes and returns one part's arrays. A program takes and returns all parts, laid end to end along the dimension named above; each array names one. Nothing has to cross between parts.
Inputs may be any that keep to these rules, and one draw needn't show every extreme that they name: `keep_list`: row h holds 96 distinct cells a * 16 + b of head h's block grid, never one with a == b. Head h keeps the first block_counts[h] cells of its keep list; one head has 96 and one has 1.
All inputs are finite; a program needn't handle non-finite values.
Results may differ from the reference program's by a relative error of at most 0.0027.
Values may be sent and summed in bfloat16 or wider, within the bound.
No kernel may reach another device: no remote copies, remote signals or barrier semaphores. Data moves between devices by JAX's collectives and lax.ppermute only.
A program may use at most 64 MiB of HBM per device.

```python
import jax
import jax.numpy as jnp
from jax import lax

DH = 128
BLK = 128
HEADS = 32
TOKENS = 2048
NB = 16
MAXB = 96


def normal_field(key, scale, bound):
    return jnp.clip(scale * jax.random.normal(key, (TOKENS, HEADS, DH), jnp.float32), -bound, bound)


def draw_queries(key, part):
    key = jax.random.fold_in(key, 3)
    samples = normal_field(key, 1.6, 9.0)
    return samples.reshape(TOKENS, HEADS * DH).astype(jnp.bfloat16)


def draw_key_vectors(key, part):
    key = jax.random.fold_in(key, 4)
    samples = normal_field(key, 1.6, 9.0)
    return samples.reshape(TOKENS, HEADS * DH).astype(jnp.bfloat16)


def draw_keep_list(key, part):
    key = jax.random.fold_in(key, 7)
    cell_total = NB * NB
    spread = max(2, 2 ** 30 // cell_total)
    scores = jax.random.randint(key, (HEADS, cell_total), 0, spread)
    cell_ids = jnp.arange(cell_total)
    diagonal = cell_ids // NB == cell_ids % NB
    ranked = jnp.where(diagonal[None, :], spread * cell_total + cell_ids[None, :], scores * cell_total + cell_ids[None, :])
    ordering = jnp.argsort(ranked, axis=1)
    return ordering[:, :MAXB].astype(jnp.int32)


def draw_block_counts(key, part):
    key = jax.random.fold_in(key, 9)
    subkeys = jax.random.split(key, 5)
    is_heavy = jax.random.randint(subkeys[0], (HEADS,), 0, 8) == 0
    light_counts = jax.random.randint(subkeys[1], (HEADS,), 1, max(2, NB * NB // 16 + 1))
    dense_counts = jax.random.randint(subkeys[2], (HEADS,), max(1, MAXB // 2), MAXB + 1)
    densest = jax.random.randint(subkeys[3], (), 0, HEADS)
    sparsest = (densest + 1 + jax.random.randint(subkeys[4], (), 0, HEADS - 1)) % HEADS
    head_ids = jnp.arange(HEADS)
    result = jnp.where(is_heavy, dense_counts, light_counts)
    result = jnp.where(head_ids == densest, MAXB, jnp.where(head_ids == sparsest, 1, result))
    return result.astype(jnp.int32)


def block_levels(stream_key, shape, shards, low, largest):
    def one(dim, parts):
        steps = jax.random.uniform(jax.random.fold_in(jax.random.fold_in(stream_key, 6), dim), (parts,), jnp.float32, low / len(shards), largest / len(shards))
        return jnp.repeat(jnp.exp(steps), shape[dim] // parts).reshape((-1,) + (1,) * (len(shape) - dim - 1))

    gain = one(*shards[0])
    for cut in shards[1:]:
        gain = gain * one(*cut)
    return gain


def gaussian(own_key, shape, deviation, reach, pieces=(), kind=jnp.bfloat16):
    values = jax.random.normal(own_key, shape, jnp.float32) * deviation
    if len(pieces) > 0:
        values = block_levels(own_key, shape, pieces, -0.22, 0.18) * values
    return jnp.clip(values, min=-reach, max=reach).astype(kind)


def setup_inputs(seed: int = 0, part: int = 0) -> dict:
    splits = jax.random.split(jax.random.key(seed), 6)
    part_keys = jax.random.split(jax.random.fold_in(splits[5], part), 6)
    queries = draw_queries(jax.random.fold_in(jax.random.fold_in(splits[5], part), 71), part)
    key_vectors = draw_key_vectors(jax.random.fold_in(jax.random.fold_in(splits[5], part), 71), part)
    value_vectors = gaussian(part_keys[2], (TOKENS, HEADS * DH), 1.0, 6.0, ((0, 16),))
    keep_list = draw_keep_list(jax.random.fold_in(jax.random.fold_in(splits[5], part), 71), part)
    block_counts = draw_block_counts(jax.random.fold_in(jax.random.fold_in(splits[5], part), 71), part)
    return dict(queries=queries, key_vectors=key_vectors, value_vectors=value_vectors, keep_list=keep_list, block_counts=block_counts)


neg_large = -1e30


def one_head(packed):
    head_queries, head_keys, head_values, head_list, head_count = packed
    live_entries = jnp.arange(MAXB) < head_count
    cell_ids = jnp.arange(NB * NB)
    listed = jnp.any((head_list[:, None] == cell_ids[None, :]) & live_entries[:, None], axis=0)
    kept = listed.reshape(NB, NB) | jnp.eye(NB, dtype=bool)
    query_tiles = head_queries.astype(jnp.float32).reshape(NB, BLK, DH)
    key_tiles = head_keys.astype(jnp.float32).reshape(NB, BLK, DH)
    value_tiles = head_values.astype(jnp.float32).reshape(NB, BLK, DH)
    scores = jnp.einsum("aid,bjd->aibj", query_tiles, key_tiles) * (DH ** -0.5)
    block_max = jnp.max(scores, axis=3)
    weights = jnp.exp(scores - block_max[..., None])
    block_total = jnp.sum(weights, axis=3)
    rounded = lax.optimization_barrier(weights.astype(jnp.bfloat16)).astype(jnp.float32)
    block_out = jnp.einsum("aibj,bjd->aibd", rounded, value_tiles)
    masked_max = jnp.where(kept[:, None, :], block_max, neg_large)
    row_max = jnp.max(masked_max, axis=2)
    factor = jnp.exp(masked_max - row_max[..., None])
    denominator = jnp.sum(factor * block_total, axis=2)
    numerator = jnp.einsum("aib,aibd->aid", factor, block_out)
    return (numerator / denominator[..., None]).reshape(NB * BLK, DH)


def by_heads(matrix):
    return jnp.transpose(matrix.reshape(TOKENS, HEADS, DH), (1, 0, 2))


def reference(queries, key_vectors, value_vectors, keep_list, block_counts):
    results = lax.map(one_head, (by_heads(queries), by_heads(key_vectors), by_heads(value_vectors), keep_list, block_counts))
    attended = jnp.transpose(results, (1, 0, 2)).reshape(TOKENS, HEADS * DH)
    return attended.astype(jnp.bfloat16)
```

```python
import functools
import math

import jax
import jax.numpy as jnp
from jax import lax
from jax.experimental import pallas as pl
from jax.experimental.pallas import tpu as pltpu
from jax.sharding import PartitionSpec as P

BLK = 128
GROUP = 4
neg_large = -1e30


def cell_partial(keys, queries, values_t, factor):
    scores = lax.dot_general(
        keys, queries, (((1,), (1,)), ((), ())), preferred_element_type=jnp.float32
    )
    scores = scores * factor
    block_max = jnp.max(scores, axis=0, keepdims=True)
    weights = jnp.exp2(scores - block_max)
    block_total = jnp.sum(weights, axis=0, keepdims=True)
    block_out = lax.dot_general(
        values_t,
        weights.astype(jnp.bfloat16),
        (((1,), (0,)), ((), ())),
        preferred_element_type=jnp.float32,
    )
    return block_max, block_total, block_out


def head_kernel(factor, cells, count, tiles, out, acc, row_max, row_total):
    nblocks = tiles.shape[0]
    live = count[0]

    for row in range(0, nblocks, GROUP):
        for a in range(row, row + GROUP):
            block_max, block_total, block_out = cell_partial(
                tiles[a, 1], tiles[a, 0], tiles[a, 2], factor
            )
            acc[a] = block_out
            row_max[a] = block_max
            row_total[a] = block_total

    def step(index, carry):
        partials = []
        for slot in range(GROUP):
            entry = index * GROUP + slot
            cell = cells[jnp.minimum(entry, live - 1)]
            a = lax.shift_right_logical(cell, 4)
            b = lax.bitwise_and(cell, 15)
            block_max, block_total, block_out = cell_partial(
                tiles[b, 1], tiles[a, 0], tiles[b, 2], factor
            )
            block_max = jnp.where(entry < live, block_max, neg_large)
            partials.append((a, block_max, block_total, block_out))
        for a, block_max, block_total, block_out in partials:
            old_max = row_max[a]
            new_max = jnp.maximum(old_max, block_max)
            rescale = jnp.exp2(old_max - new_max)
            share = jnp.exp2(block_max - new_max)
            row_max[a] = new_max
            row_total[a] = row_total[a] * rescale + block_total * share
            acc[a] = acc[a] * rescale + block_out * share
        return carry

    lax.fori_loop(0, (live + GROUP - 1) // GROUP, step, 0)

    for a in range(nblocks):
        out[a] = (acc[a] / row_total[a]).T.astype(out.dtype)


def attend(tiles, cells, count, name):
    nblocks, _, rows, head_dim = tiles.shape
    factor = head_dim ** (-0.5) * math.log2(math.e)
    vmem = pl.BlockSpec(memory_space=pltpu.VMEM)
    smem = pl.BlockSpec(memory_space=pltpu.SMEM)
    return pl.pallas_call(
        functools.partial(head_kernel, factor),
        out_shape=jax.ShapeDtypeStruct((nblocks, rows, head_dim), jnp.bfloat16),
        in_specs=[smem, smem, vmem],
        out_specs=vmem,
        scratch_shapes=[
            pltpu.VMEM((nblocks, head_dim, rows), jnp.float32),
            pltpu.VMEM((nblocks, 1, rows), jnp.float32),
            pltpu.VMEM((nblocks, 1, rows), jnp.float32),
        ],
        compiler_params=pltpu.CompilerParams(vmem_limit_bytes=16 * 1024 * 1024),
        cost_estimate=pl.CostEstimate(
            flops=4 * 64 * rows * rows * head_dim,
            bytes_accessed=2 * 4 * nblocks * rows * head_dim,
            transcendentals=64 * rows * rows,
        ),
        name=name,
    )(cells, count, tiles)


def on_device(queries, key_vectors, value_vectors, keep_list, block_counts):
    peers = lax.axis_size("seq")
    me = lax.axis_index("seq")
    head_total = block_counts.shape[0]
    heads_here = head_total // peers
    head_dim = queries.shape[1] // head_total
    tok_local = queries.shape[0]
    split = (tok_local, peers, heads_here, head_dim)
    q = queries.reshape(split)
    k = key_vectors.reshape(split)
    v = value_vectors.reshape(split)
    counts = lax.dynamic_slice(block_counts, (me * heads_here,), (heads_here,))

    results = []
    for j in range(heads_here):
        packed = jnp.stack(
            [
                q[:, :, j].transpose(1, 0, 2),
                k[:, :, j].transpose(1, 0, 2),
                v[:, :, j].transpose(1, 2, 0),
            ],
            axis=1,
        )
        tiles = lax.all_to_all(packed, "seq", split_axis=0, concat_axis=0, tiled=True)
        attended = attend(tiles, keep_list[j], counts[j : j + 1], f"head_{j}")
        results.append(lax.all_to_all(attended, "seq", split_axis=0, concat_axis=0, tiled=True))
    together = jnp.stack(results, axis=0)
    return together.transpose(2, 1, 0, 3).reshape(tok_local, head_total * head_dim)


def solution(mesh):
    tokens = P(("batch", "seq"), None)
    return jax.shard_map(
        on_device,
        mesh=mesh,
        in_specs=(tokens, tokens, tokens, tokens, P("batch")),
        out_specs=tokens,
        check_vma=False,
    )
```

```python
import functools
import math

import jax
import jax.numpy as jnp
from jax import lax
from jax.experimental import pallas as pl
from jax.experimental.pallas import tpu as pltpu
from jax.sharding import PartitionSpec as P

GROUP = 8
neg_large = -1e30
NT = (((1,), (1,)), ((), ()))
NN = (((1,), (0,)), ((), ()))
VMEM = pl.BlockSpec(memory_space=pltpu.VMEM)
SMEM = pl.BlockSpec(memory_space=pltpu.SMEM)
ANY = pl.BlockSpec(memory_space=pl.ANY)


def pack_kernel(first, stride, queries, keys, values, packed, sem):
    peers, _, _, head_dim = packed.shape
    for peer in range(peers):
        column = (peer * stride + first) * head_dim
        for which, source in enumerate((queries, keys, values)):
            pltpu.make_async_copy(
                source.at[:, pl.ds(column, head_dim)], packed.at[peer, which], sem
            ).start()
    pltpu.make_async_copy(packed, packed, sem).wait()


def pack(queries, keys, values, first, stride, peers, head_dim):
    rows = queries.shape[0]
    return pl.pallas_call(
        functools.partial(pack_kernel, first, stride),
        out_shape=jax.ShapeDtypeStruct((peers, 3, rows, head_dim), queries.dtype),
        in_specs=[ANY, ANY, ANY],
        out_specs=ANY,
        scratch_shapes=[pltpu.SemaphoreType.DMA],
        cost_estimate=pl.CostEstimate(
            flops=0, bytes_accessed=6 * peers * 2 * rows * head_dim, transcendentals=0
        ),
        name=f"pack_{first}",
    )(queries, keys, values)


def unpack_kernel(*refs):
    heads, out = refs[:-1], refs[-1]
    peers, _, head_dim = heads[0].shape
    for peer in range(peers):
        for j, head in enumerate(heads):
            column = (peer * len(heads) + j) * head_dim
            out[:, column : column + head_dim] = head[peer]


def unpack(heads):
    peers, rows, head_dim = heads[0].shape
    columns = len(heads) * peers * head_dim
    steps = 4
    return pl.pallas_call(
        unpack_kernel,
        grid=(steps,),
        out_shape=jax.ShapeDtypeStruct((rows, columns), heads[0].dtype),
        in_specs=[pl.BlockSpec((peers // steps, rows, head_dim), lambda i: (i, 0, 0))] * len(heads),
        out_specs=pl.BlockSpec((rows, columns // steps), lambda i: (0, i)),
        name="unpack",
    )(*heads)


def head_kernel(factor, cells, count, tiles, out, values_t, held, held_max, acc, row_max, row_total):
    nblocks = tiles.shape[0]
    live = count[0]

    def score(slot, a, b):
        scores = factor * lax.dot_general(
            tiles[b, 1], tiles[a, 0], NT, preferred_element_type=jnp.float32
        )
        block_max = jnp.max(scores, axis=0, keepdims=True)
        held[slot] = scores
        held_max[slot] = block_max
        return block_max

    def weigh(slot, a, b, is_live):
        block_max = held_max[slot]
        weights = jnp.exp2(held[slot] - block_max)
        share = jnp.exp2(block_max - row_max[a])
        if is_live is not None:
            share = jnp.where(is_live, share, 0.0)
        block_total = jnp.sum(weights, axis=0, keepdims=True)
        block_out = lax.dot_general(
            values_t[b], weights.astype(jnp.bfloat16), NN, preferred_element_type=jnp.float32
        )
        return share * block_total, share * block_out

    def locate(entry):
        cell = cells[jnp.minimum(entry, live - 1)]
        return lax.shift_right_logical(cell, 4), lax.bitwise_and(cell, 15)

    for a in range(nblocks):
        row_max[a] = score(a, a, a)
        values_t[a] = tiles[a, 2].T

    def first_pass(index, carry):
        found = []
        for entry in [index * GROUP + lane for lane in range(GROUP)]:
            a, b = locate(entry)
            found.append((a, score(nblocks + entry, a, b)))
        for a, block_max in found:
            row_max[a] = jnp.maximum(row_max[a], block_max)
        return carry

    steps = (live + GROUP - 1) // GROUP
    lax.fori_loop(0, steps, first_pass, 0)

    for a in range(nblocks):
        row_total[a], acc[a] = weigh(a, a, a, None)

    def second_pass(index, carry):
        found = []
        for entry in [index * GROUP + lane for lane in range(GROUP)]:
            a, b = locate(entry)
            found.append((a, *weigh(nblocks + entry, a, b, entry < live)))
        for a, total, product in found:
            row_total[a] += total
            acc[a] += product
        return carry

    lax.fori_loop(0, steps, second_pass, 0)

    for a in range(nblocks):
        out[a] = (acc[a] / row_total[a]).T.astype(out.dtype)


def attend(tiles, cells, count, name):
    nblocks, _, rows, head_dim = tiles.shape
    factor = head_dim ** (-0.5) * math.log2(math.e)
    slots = nblocks + -(-cells.shape[0] // GROUP) * GROUP
    return pl.pallas_call(
        functools.partial(head_kernel, factor),
        out_shape=jax.ShapeDtypeStruct((nblocks, rows, head_dim), jnp.bfloat16),
        in_specs=[SMEM, SMEM, VMEM],
        out_specs=VMEM,
        scratch_shapes=[
            pltpu.VMEM((nblocks, head_dim, rows), jnp.bfloat16),
            pltpu.VMEM((slots, rows, rows), jnp.float32),
            pltpu.VMEM((slots, 1, rows), jnp.float32),
            pltpu.VMEM((nblocks, head_dim, rows), jnp.float32),
            pltpu.VMEM((nblocks, 1, rows), jnp.float32),
            pltpu.VMEM((nblocks, 1, rows), jnp.float32),
        ],
        compiler_params=pltpu.CompilerParams(vmem_limit_bytes=24 * 1024 * 1024),
        cost_estimate=pl.CostEstimate(
            flops=4 * 64 * rows * rows * head_dim,
            bytes_accessed=2 * 4 * nblocks * rows * head_dim,
            transcendentals=64 * rows * rows,
        ),
        name=name,
    )(cells, count, tiles)


def on_device(queries, key_vectors, value_vectors, keep_list, block_counts):
    peers = lax.axis_size("seq")
    me = lax.axis_index("seq")
    head_total = block_counts.shape[0]
    heads_here = head_total // peers
    head_dim = queries.shape[1] // head_total
    counts = lax.dynamic_slice(block_counts, (me * heads_here,), (heads_here,))

    results = []
    for j in range(heads_here):
        packed = pack(queries, key_vectors, value_vectors, j, heads_here, peers, head_dim)
        tiles = lax.all_to_all(packed, "seq", split_axis=0, concat_axis=0, tiled=True)
        attended = attend(tiles, keep_list[j], counts[j : j + 1], f"head_{j}")
        results.append(lax.all_to_all(attended, "seq", split_axis=0, concat_axis=0, tiled=True))
    return unpack(results)


def solution(mesh):
    tokens = P(("batch", "seq"), None)
    return jax.shard_map(
        on_device,
        mesh=mesh,
        in_specs=(tokens, tokens, tokens, tokens, P("batch")),
        out_specs=tokens,
        check_vma=False,
    )
```

```python
import functools
import math

import jax
import jax.numpy as jnp
from jax import lax
from jax.experimental import pallas as pl
from jax.experimental.pallas import tpu as pltpu
from jax.sharding import PartitionSpec as P

GROUP = 8
CHUNKS = 8
KINDS = 3
LIST_ROWS = 16
NT = (((1,), (1,)), ((), ()))
NN = (((1,), (0,)), ((), ()))
VMEM = pl.BlockSpec(memory_space=pltpu.VMEM)
SMEM = pl.BlockSpec(memory_space=pltpu.SMEM)
ANY = pl.BlockSpec(memory_space=pl.ANY)


def rank_to_place(rank, peers):
    j = rank // peers
    peer = rank - j * peers
    return jnp.where(j % 2 == 0, peer, peers - 1 - peer), j


def place_to_rank(peer, j, peers):
    return j * peers + (peer if j % 2 == 0 else peers - 1 - peer)


def tile_rows(j, kind, rows):
    return pl.ds(pl.multiple_of((j * KINDS + kind) * rows, rows), rows)


def pack_kernel(
    counts, lists, queries, keys, values, packed, order, came, goes, gone_lists, list_tile_ref, keys_of, ranks, came_sems, goes_sem
):
    peers, _, head_dim = packed.shape
    head_total = counts.shape[0]
    rows = queries.shape[0]
    per_chunk = head_total // CHUNKS
    sources = (queries, keys, values)
    copies = []
    for chunk in range(CHUNKS):
        span = pl.ds(chunk * per_chunk * head_dim, per_chunk * head_dim)
        for kind, source in enumerate(sources):
            copy = pltpu.make_async_copy(
                source.at[:, span], came.at[kind, :, span], came_sems.at[chunk, kind]
            )
            copy.start()
            copies.append(copy)

    gone_lists[...] = jnp.zeros_like(gone_lists)
    gone_lists[: lists.shape[0], : lists.shape[1]] = lists[...].astype(jnp.float32)
    list_tile_ref[...] = gone_lists[...].astype(packed.dtype)
    for peer in range(peers):
        pltpu.make_async_copy(
            list_tile_ref, packed.at[peer, pl.ds(head_total // peers * KINDS * rows, LIST_ROWS)], goes_sem
        ).start()

    for head in range(head_total):
        keys_of[head] = counts[head] * head_total - head

    def find_rank(head, carry):
        mine = keys_of[head]
        rank = jnp.int32(0)
        for other in range(head_total):
            rank += (keys_of[other] > mine).astype(jnp.int32)
        ranks[head] = rank
        order[rank] = head
        return carry

    lax.fori_loop(0, head_total, find_rank, 0)

    for head in range(head_total):
        chunk, first = divmod(head, per_chunk)
        for kind in range(len(sources)):
            if first == 0:
                copies[chunk * len(sources) + kind].wait()
            goes[head, kind * rows : (kind + 1) * rows] = came[
                kind, :, head * head_dim : (head + 1) * head_dim
            ]
        peer, j = rank_to_place(ranks[head], peers)
        span = pl.ds(pl.multiple_of(j * KINDS * rows, rows), KINDS * rows)
        pltpu.make_async_copy(goes.at[head], packed.at[peer, span], goes_sem).start()
    pltpu.make_async_copy(packed, packed, goes_sem).wait()


def pack(counts, lists, queries, keys, values, peers):
    rows, columns = queries.shape
    head_total = counts.shape[0]
    head_dim = columns // head_total
    heads_here = head_total // peers
    parcel_rows = heads_here * KINDS * rows + LIST_ROWS
    return pl.pallas_call(
        pack_kernel,
        out_shape=(
            jax.ShapeDtypeStruct((peers, parcel_rows, head_dim), queries.dtype),
            jax.ShapeDtypeStruct((head_total,), jnp.int32),
        ),
        in_specs=[SMEM, VMEM, ANY, ANY, ANY],
        out_specs=(ANY, SMEM),
        scratch_shapes=[
            pltpu.VMEM((KINDS, rows, columns), queries.dtype),
            pltpu.VMEM((head_total, KINDS * rows, head_dim), queries.dtype),
            pltpu.VMEM((LIST_ROWS, head_dim), jnp.float32),
            pltpu.VMEM((LIST_ROWS, head_dim), queries.dtype),
            pltpu.SMEM((head_total,), jnp.int32),
            pltpu.SMEM((head_total,), jnp.int32),
            pltpu.SemaphoreType.DMA((CHUNKS, KINDS)),
            pltpu.SemaphoreType.DMA,
        ],
        compiler_params=pltpu.CompilerParams(vmem_limit_bytes=60 * 1024 * 1024),
        name="pack",
    )(counts, lists, queries, keys, values)


def unpack_kernel(order, heads, out, staged, sems):
    peers, heads_here, rows, head_dim = heads.shape
    step = rows // CHUNKS
    copies = []
    for chunk in range(CHUNKS):
        span = pl.ds(chunk * step, step)
        for peer in range(peers):
            for j in range(heads_here):
                head = order[place_to_rank(peer, j, peers)]
                column = pl.multiple_of(head * head_dim, head_dim)
                staged[span, pl.ds(column, head_dim)] = heads[peer, j, span, :]
        copy = pltpu.make_async_copy(staged.at[span, :], out.at[span, :], sems.at[chunk])
        copy.start()
        copies.append(copy)
    for copy in copies:
        copy.wait()


def unpack(order, heads):
    peers, heads_here, rows, head_dim = heads.shape
    columns = peers * heads_here * head_dim
    return pl.pallas_call(
        unpack_kernel,
        out_shape=jax.ShapeDtypeStruct((rows, columns), heads.dtype),
        in_specs=[SMEM, VMEM],
        out_specs=ANY,
        scratch_shapes=[
            pltpu.VMEM((rows, columns), heads.dtype),
            pltpu.SemaphoreType.DMA((CHUNKS,)),
        ],
        compiler_params=pltpu.CompilerParams(vmem_limit_bytes=8 * 1024 * 1024),
        name="unpack",
    )(order, heads)


def heads_kernel(
    factor,
    me,
    order,
    all_counts,
    parcels,
    out,
    values_t,
    held,
    held_max,
    acc,
    row_max,
    row_total,
    came_lists,
    cells,
    lists_sem,
):
    nblocks, heads_here, rows, _ = out.shape
    grid_rows = nblocks * heads_here
    peers = order.shape[0] // heads_here
    lists_at = heads_here * KINDS * rows
    for sender in range(peers):
        numbers = parcels[sender, pl.ds(lists_at, LIST_ROWS), :].astype(jnp.float32)
        came_lists[pl.ds(sender * 8, 8)] = numbers[:8].astype(jnp.int32)
    lists_copy = pltpu.make_async_copy(came_lists, cells, lists_sem)
    lists_copy.start()
    heads = [order[place_to_rank(me[0], j, peers)] for j in range(heads_here)]
    counts = [all_counts[head] for head in heads]
    live = functools.reduce(lambda x, y: x + y, counts)

    def score(slot, j, a, b):
        scores = factor * lax.dot_general(
            parcels[b, tile_rows(j, 1, rows), :],
            parcels[a, tile_rows(j, 0, rows), :],
            NT,
            preferred_element_type=jnp.float32,
        )
        block_max = jnp.max(scores, axis=0, keepdims=True)
        held[slot] = scores
        held_max[slot] = block_max
        return block_max

    def weigh(slot, j, a, b, is_live):
        block_max = held_max[slot]
        weights = jnp.exp2(held[slot] - block_max)
        share = jnp.exp2(block_max - row_max[j * nblocks + a])
        if is_live is not None:
            share = jnp.where(is_live, share, 0.0)
        block_total = jnp.sum(weights, axis=0, keepdims=True)
        block_out = lax.dot_general(
            values_t[j * nblocks + b],
            weights.astype(jnp.bfloat16),
            NN,
            preferred_element_type=jnp.float32,
        )
        return share * block_total, share * block_out

    def locate(entry):
        entry = jnp.minimum(entry, live - 1)
        j = jnp.int32(0)
        head = heads[0]
        place = entry
        for later in range(1, heads_here):
            entry -= counts[later - 1]
            j = jnp.where(entry >= 0, later, j)
            head = jnp.where(entry >= 0, heads[later], head)
            place = jnp.where(entry >= 0, entry, place)
        sender = head // heads_here
        cell = cells[sender * 8 + (head - sender * heads_here), place]
        return j, lax.shift_right_logical(cell, 4), lax.bitwise_and(cell, 15)

    for j in range(heads_here):
        for a in range(nblocks):
            row = j * nblocks + a
            row_max[row] = score(row, j, a, a)
            values_t[row] = parcels[a, tile_rows(j, 2, rows), :].T

    def first_pass(index, carry):
        found = []
        for entry in [index * GROUP + lane for lane in range(GROUP)]:
            j, a, b = locate(entry)
            found.append((j * nblocks + a, score(grid_rows + entry, j, a, b)))
        for row, block_max in found:
            row_max[row] = jnp.maximum(row_max[row], block_max)
        return carry

    steps = (live + GROUP - 1) // GROUP
    lists_copy.wait()
    lax.fori_loop(0, steps, first_pass, 0)

    for j in range(heads_here):
        for a in range(nblocks):
            row = j * nblocks + a
            row_total[row], acc[row] = weigh(row, j, a, a, None)

    def second_pass(index, carry):
        found = []
        for entry in [index * GROUP + lane for lane in range(GROUP)]:
            j, a, b = locate(entry)
            found.append((j * nblocks + a, *weigh(grid_rows + entry, j, a, b, entry < live)))
        for row, total, product in found:
            row_total[row] += total
            acc[row] += product
        return carry

    lax.fori_loop(0, steps, second_pass, 0)

    for j in range(heads_here):
        for a in range(nblocks):
            row = j * nblocks + a
            out[a, j] = (acc[row] / row_total[row]).T.astype(out.dtype)


def attend(me, order, counts, parcels, list_len):
    nblocks, parcel_rows, head_dim = parcels.shape
    peers = nblocks
    heads_here = counts.shape[0] // peers
    rows = (parcel_rows - LIST_ROWS) // (heads_here * KINDS)
    factor = head_dim ** (-0.5) * math.log2(math.e)
    grid_rows = nblocks * heads_here
    slots = grid_rows + -(-list_len * heads_here // GROUP) * GROUP
    return pl.pallas_call(
        functools.partial(heads_kernel, factor),
        out_shape=jax.ShapeDtypeStruct((nblocks, heads_here, rows, head_dim), jnp.bfloat16),
        in_specs=[SMEM, SMEM, SMEM, VMEM],
        out_specs=VMEM,
        scratch_shapes=[
            pltpu.VMEM((grid_rows, head_dim, rows), jnp.bfloat16),
            pltpu.VMEM((slots, rows, rows), jnp.float32),
            pltpu.VMEM((slots, 1, rows), jnp.float32),
            pltpu.VMEM((grid_rows, head_dim, rows), jnp.float32),
            pltpu.VMEM((grid_rows, 1, rows), jnp.float32),
            pltpu.VMEM((grid_rows, 1, rows), jnp.float32),
            pltpu.VMEM((peers * 8, head_dim), jnp.int32),
            pltpu.SMEM((peers * 8, head_dim), jnp.int32),
            pltpu.SemaphoreType.DMA,
        ],
        compiler_params=pltpu.CompilerParams(vmem_limit_bytes=36 * 1024 * 1024),
        name="attend",
    )(me, order, counts, parcels)


def on_device(queries, key_vectors, value_vectors, keep_list, block_counts):
    peers = lax.axis_size("seq")
    me = lax.axis_index("seq")
    packed, order = pack(
        block_counts, keep_list, queries, key_vectors, value_vectors, peers
    )
    parcels = lax.all_to_all(packed, "seq", split_axis=0, concat_axis=0, tiled=True)
    attended = attend(me.reshape(1), order, block_counts, parcels, keep_list.shape[1])
    returned = lax.all_to_all(attended, "seq", split_axis=0, concat_axis=0, tiled=True)
    return unpack(order, returned)


def solution(mesh):
    tokens = P(("batch", "seq"), None)
    return jax.shard_map(
        on_device,
        mesh=mesh,
        in_specs=(tokens, tokens, tokens, tokens, P("batch")),
        out_specs=tokens,
        check_vma=False,
    )
```

```python
import functools
import math

import jax
import jax.numpy as jnp
from jax import lax
from jax.experimental import pallas as pl
from jax.experimental.pallas import tpu as pltpu
from jax.sharding import PartitionSpec as P

GROUP = 16
NONE = 16
CHUNKS = 8
LOADS = 4
KINDS = 3
PAIR_ROWS = 8
LIST_ROWS = 16
NT = (((1,), (1,)), ((), ()))
NN = (((1,), (0,)), ((), ()))
VMEM = pl.BlockSpec(memory_space=pltpu.VMEM)
SMEM = pl.BlockSpec(memory_space=pltpu.SMEM)
ANY = pl.BlockSpec(memory_space=pl.ANY)


def rank_to_place(rank, peers):
    j = rank // peers
    peer = rank - j * peers
    return jnp.where(j % 2 == 0, peer, peers - 1 - peer), j


def place_to_rank(peer, j, peers):
    return j * peers + (peer if j % 2 == 0 else peers - 1 - peer)


def tile_rows(j, kind, rows):
    return pl.ds(pl.multiple_of((j * KINDS + kind) * rows, rows), rows)


def small_product(left, right):
    return jnp.dot(
        left.astype(jnp.bfloat16), right.astype(jnp.bfloat16), preferred_element_type=jnp.float32
    )


def pair_tables(lists, list_len, live):
    lines, size = lists.shape
    across = lax.broadcasted_iota(jnp.int32, (size, size), 1)
    down = lax.broadcasted_iota(jnp.int32, (size, size), 0)
    lane = lax.broadcasted_iota(jnp.int32, (lines, size), 1)
    line = lax.broadcasted_iota(jnp.int32, (lines, size), 0)
    across_f = across.astype(jnp.float32)
    on_diagonal = (lane >= list_len) & (lane < list_len + 16)
    cell = jnp.where(on_diagonal, (lane - list_len) * 17, lists)
    listed = functools.reduce(lambda x, y: x | y, [(line == j) & (lane < c) for j, c in enumerate(live)])
    row = lax.shift_right_logical(cell, 4).astype(jnp.float32)
    column = jnp.where(on_diagonal | listed, lax.bitwise_and(cell, 15), size).astype(jnp.float32)
    upright = jnp.concatenate([column, row, jnp.zeros((size - 2 * lines, size), jnp.float32)], axis=0).T
    members = [(upright[:, j : j + 1] == across_f).astype(jnp.float32) for j in range(len(live))]
    counted = small_product((across < down).astype(jnp.float32), jnp.concatenate(members, axis=1))
    pairs = [jnp.floor((jnp.sum(member, axis=0, keepdims=True) + 1.0) * 0.5) for member in members]
    pairs_lines = functools.reduce(
        lambda x, y: x + y, [jnp.where(line == j, p, 0.0) for j, p in enumerate(pairs)]
    )
    firsts = small_product(pairs_lines, (down < across).astype(jnp.float32))
    tables = []
    for j, member in enumerate(members):
        earlier = jnp.sum(member * counted[:, j * size : (j + 1) * size], axis=1, keepdims=True)
        half = jnp.floor(earlier * 0.5)
        place = jnp.sum(member * firsts[j : j + 1], axis=1, keepdims=True) + half
        here = jnp.where(place == across_f, jnp.sum(member, axis=1, keepdims=True), 0.0)
        second = earlier - 2.0 * half
        picks = jnp.concatenate([here * (1.0 - second), here * second], axis=1)
        own_column, own_row = column[j : j + 1], row[j : j + 1]
        facts = jnp.where(line == 0, own_column, jnp.where(line == 1, own_row, own_row - NONE))
        found = small_product(facts, picks)
        total = jnp.sum(pairs[j], axis=1, keepdims=True)
        tables.append(
            jnp.where(
                line < 2, found[:, :size], jnp.where(line == 2, found[:, size:] + NONE, total)
            )
        )
    return jnp.concatenate(tables, axis=0)


def pack_kernel(
    me, counts, lists, queries, keys, values, packed, order, came, goes, wide_lists, gone_tables, came_sems, goes_sem
):
    peers, _, head_dim = packed.shape
    head_total = counts.shape[0]
    rows = queries.shape[0]
    per_chunk = head_total // LOADS
    sources = (queries, keys, values)
    copies = []
    for chunk in range(LOADS):
        span = pl.ds(chunk * per_chunk * head_dim, per_chunk * head_dim)
        for kind, source in enumerate(sources):
            copy = pltpu.make_async_copy(
                source.at[:, span], came.at[kind, :, span], came_sems.at[chunk, kind]
            )
            copy.start()
            copies.append(copy)

    heads_here = head_total // peers

    def send_tables():
        live = [counts[me[0] * heads_here + j] for j in range(heads_here)]
        wide_lists[...] = jnp.zeros_like(wide_lists)
        wide_lists[:heads_here, : lists.shape[1]] = lists[...]
        tables = pair_tables(wide_lists[...], lists.shape[1], live).astype(packed.dtype)
        for peer in range(peers):
            gone_tables[peer] = tables
        pltpu.make_async_copy(
            gone_tables, packed.at[:, pl.ds(heads_here * KINDS * rows, LIST_ROWS)], goes_sem
        ).start()

    weights = [counts[head] * head_total - head for head in range(head_total)]
    ranks = [jnp.int32(0)] * head_total
    for head in range(head_total):
        for other in range(head):
            ahead = (weights[other] > weights[head]).astype(jnp.int32)
            ranks[head] += ahead
            ranks[other] += 1 - ahead
    for head, rank in enumerate(ranks):
        order[rank] = head

    for head in range(head_total):
        if head == 0:
            send_tables()
        chunk, first = divmod(head, per_chunk)
        for kind in range(len(sources)):
            if first == 0:
                copies[chunk * len(sources) + kind].wait()
            goes[head, kind * rows : (kind + 1) * rows] = came[
                kind, :, head * head_dim : (head + 1) * head_dim
            ]
        peer, j = rank_to_place(ranks[head], peers)
        span = pl.ds(pl.multiple_of(j * KINDS * rows, rows), KINDS * rows)
        pltpu.make_async_copy(goes.at[head], packed.at[peer, span], goes_sem).start()
    pltpu.make_async_copy(packed, packed, goes_sem).wait()


def pack(me, counts, lists, queries, keys, values, peers):
    rows, columns = queries.shape
    head_total = counts.shape[0]
    head_dim = columns // head_total
    heads_here = head_total // peers
    parcel_rows = heads_here * KINDS * rows + LIST_ROWS
    return pl.pallas_call(
        pack_kernel,
        out_shape=(
            jax.ShapeDtypeStruct((peers, parcel_rows, head_dim), queries.dtype),
            jax.ShapeDtypeStruct((head_total,), jnp.int32),
        ),
        in_specs=[SMEM, SMEM, VMEM, ANY, ANY, ANY],
        out_specs=(ANY, SMEM),
        scratch_shapes=[
            pltpu.VMEM((KINDS, rows, columns), queries.dtype),
            pltpu.VMEM((head_total, KINDS * rows, head_dim), queries.dtype),
            pltpu.VMEM((PAIR_ROWS, head_dim), jnp.int32),
            pltpu.VMEM((peers, LIST_ROWS, head_dim), queries.dtype),
            pltpu.SemaphoreType.DMA((LOADS, KINDS)),
            pltpu.SemaphoreType.DMA,
        ],
        compiler_params=pltpu.CompilerParams(vmem_limit_bytes=60 * 1024 * 1024),
        name="pack",
    )(me, counts, lists, queries, keys, values)


def unpack_kernel(order, heads, out, staged, sems):
    peers, heads_here, rows, head_dim = heads.shape
    step = rows // CHUNKS
    copies = []
    for chunk in range(CHUNKS):
        span = pl.ds(chunk * step, step)
        for peer in range(peers):
            for j in range(heads_here):
                head = order[place_to_rank(peer, j, peers)]
                column = pl.multiple_of(head * head_dim, head_dim)
                staged[span, pl.ds(column, head_dim)] = heads[peer, j, span, :]
        copy = pltpu.make_async_copy(staged.at[span, :], out.at[span, :], sems.at[chunk])
        copy.start()
        copies.append(copy)
    for copy in copies:
        copy.wait()


def unpack(order, heads):
    peers, heads_here, rows, head_dim = heads.shape
    columns = peers * heads_here * head_dim
    return pl.pallas_call(
        unpack_kernel,
        out_shape=jax.ShapeDtypeStruct((rows, columns), heads.dtype),
        in_specs=[SMEM, VMEM],
        out_specs=ANY,
        scratch_shapes=[
            pltpu.VMEM((rows, columns), heads.dtype),
            pltpu.SemaphoreType.DMA((CHUNKS,)),
        ],
        compiler_params=pltpu.CompilerParams(vmem_limit_bytes=8 * 1024 * 1024),
        name="unpack",
    )(order, heads)


def heads_kernel(
    factor, me, order, parcels, out, values_t, held, held_max, acc, row_max, row_total, came_tables, tables, tables_sem
):
    nblocks, heads_here, rows, _ = out.shape
    peers = order.shape[0] // heads_here
    starts = []
    for j in range(heads_here):
        head = order[place_to_rank(me[0], j, peers)]
        sender = lax.div(head, heads_here)
        numbers = parcels[sender, pl.ds(heads_here * KINDS * rows, LIST_ROWS), :]
        came_tables[j * LIST_ROWS : (j + 1) * LIST_ROWS] = numbers.astype(jnp.float32).astype(jnp.int32)
        starts.append(j * LIST_ROWS + (head - sender * heads_here) * PAIR_ROWS)
    tables_copy = pltpu.make_async_copy(came_tables, tables, tables_sem)
    tables_copy.start()

    for j in range(heads_here):
        for a in range(nblocks):
            row = j * nblocks + a
            values_t[row] = parcels[a, tile_rows(j, 2, rows), :].T
            acc[row] = jnp.zeros_like(acc[row])
    row_max[...] = jnp.full_like(row_max, -jnp.inf)
    row_total[...] = jnp.zeros_like(row_total)

    tables_copy.wait()
    pairs = [tables[start + 3, 0] for start in starts]
    live = functools.reduce(lambda x, y: x + y, pairs)

    def locate(entry):
        entry = jnp.minimum(entry, live - 1)
        j = jnp.int32(0)
        start, place = starts[0], entry
        for later in range(1, heads_here):
            entry -= pairs[later - 1]
            j = jnp.where(entry >= 0, later, j)
            start = jnp.where(entry >= 0, starts[later], start)
            place = jnp.where(entry >= 0, entry, place)
        b, one, two = (tables[start + line, place] for line in range(3))
        return j, b, one, jnp.where(two == NONE, one, two), two != NONE

    def first_pass(index, carry):
        found = []
        for entry in [index * GROUP + lane for lane in range(GROUP)]:
            j, b, one, two, _ = locate(entry)
            both = jnp.concatenate(
                [parcels[one, tile_rows(j, 0, rows), :], parcels[two, tile_rows(j, 0, rows), :]], axis=0
            )
            scores = factor * lax.dot_general(
                parcels[b, tile_rows(j, 1, rows), :], both, NT, preferred_element_type=jnp.float32
            )
            block_max = jnp.max(scores, axis=0, keepdims=True)
            held[entry] = scores
            held_max[entry] = block_max
            found.append((j * nblocks + one, block_max[:, :rows]))
            found.append((j * nblocks + two, block_max[:, rows:]))
        for row, block_max in found:
            row_max[row] = jnp.maximum(row_max[row], block_max)
        return carry

    steps = (live + GROUP - 1) // GROUP
    lax.fori_loop(0, steps, first_pass, 0)

    def second_pass(index, carry):
        found = []
        for entry in [index * GROUP + lane for lane in range(GROUP)]:
            j, b, one, two, is_two = locate(entry)
            one, two = j * nblocks + one, j * nblocks + two
            block_max = held_max[entry]
            weights = jnp.exp2(held[entry] - block_max)
            is_live = entry < live
            share = jnp.concatenate(
                [
                    jnp.where(is_live, jnp.exp2(block_max[:, :rows] - row_max[one]), 0.0),
                    jnp.where(is_live & is_two, jnp.exp2(block_max[:, rows:] - row_max[two]), 0.0),
                ],
                axis=1,
            )
            total = share * jnp.sum(weights, axis=0, keepdims=True)
            product = share * lax.dot_general(
                values_t[j * nblocks + b],
                weights.astype(jnp.bfloat16),
                NN,
                preferred_element_type=jnp.float32,
            )
            found.append((one, total[:, :rows], product[:, :rows]))
            found.append((two, total[:, rows:], product[:, rows:]))
        for row, total, product in found:
            row_total[row] += total
            acc[row] += product
        return carry

    lax.fori_loop(0, steps, second_pass, 0)

    for j in range(heads_here):
        for a in range(nblocks):
            row = j * nblocks + a
            out[a, j] = (acc[row] * (1.0 / row_total[row])).T.astype(out.dtype)


def attend(me, order, parcels, list_len):
    nblocks, parcel_rows, head_dim = parcels.shape
    heads_here = order.shape[0] // nblocks
    rows = (parcel_rows - LIST_ROWS) // (heads_here * KINDS)
    factor = head_dim ** (-0.5) * math.log2(math.e)
    grid_rows = nblocks * heads_here
    slots = -(-heads_here * (list_len + 2 * nblocks) // (2 * GROUP)) * GROUP
    return pl.pallas_call(
        functools.partial(heads_kernel, factor),
        out_shape=jax.ShapeDtypeStruct((nblocks, heads_here, rows, head_dim), jnp.bfloat16),
        in_specs=[SMEM, SMEM, VMEM],
        out_specs=VMEM,
        scratch_shapes=[
            pltpu.VMEM((grid_rows, head_dim, rows), jnp.bfloat16),
            pltpu.VMEM((slots, rows, 2 * rows), jnp.float32),
            pltpu.VMEM((slots, 1, 2 * rows), jnp.float32),
            pltpu.VMEM((grid_rows, head_dim, rows), jnp.float32),
            pltpu.VMEM((grid_rows, 1, rows), jnp.float32),
            pltpu.VMEM((grid_rows, 1, rows), jnp.float32),
            pltpu.VMEM((heads_here * LIST_ROWS, head_dim), jnp.int32),
            pltpu.SMEM((heads_here * LIST_ROWS, head_dim), jnp.int32),
            pltpu.SemaphoreType.DMA,
        ],
        compiler_params=pltpu.CompilerParams(vmem_limit_bytes=36 * 1024 * 1024),
        name="attend",
    )(me, order, parcels)


def on_device(queries, key_vectors, value_vectors, keep_list, block_counts):
    peers = lax.axis_size("seq")
    me = lax.axis_index("seq").reshape(1)
    packed, order = pack(me, block_counts, keep_list, queries, key_vectors, value_vectors, peers)
    parcels = lax.all_to_all(packed, "seq", split_axis=0, concat_axis=0, tiled=True)
    attended = attend(me, order, parcels, keep_list.shape[1])
    returned = lax.all_to_all(attended, "seq", split_axis=0, concat_axis=0, tiled=True)
    return unpack(order, returned)


def solution(mesh):
    tokens = P(("batch", "seq"), None)
    return jax.shard_map(
        on_device,
        mesh=mesh,
        in_specs=(tokens, tokens, tokens, tokens, P("batch")),
        out_specs=tokens,
        check_vma=False,
    )
```

```python
import functools
import math

import jax
import jax.numpy as jnp
from jax import lax
from jax.experimental import pallas as pl
from jax.experimental.pallas import tpu as pltpu
from jax.sharding import PartitionSpec as P

GROUP = 16
NONE = 16
CHUNKS = 8
LOADS = 4
KINDS = 3
PAIR_ROWS = 8
NT = (((1,), (1,)), ((), ()))
NN = (((1,), (0,)), ((), ()))
VMEM = pl.BlockSpec(memory_space=pltpu.VMEM)
SMEM = pl.BlockSpec(memory_space=pltpu.SMEM)
ANY = pl.BlockSpec(memory_space=pl.ANY)


CORES = 2


def rank_to_place(rank, heads_here):
    j = lax.div(rank, CORES)
    core = rank - j * CORES
    return jnp.where(lax.rem(j, 2) == 0, core, CORES - 1 - core), j


def place_to_slot(peer, j, heads_here):
    chip = lax.div(peer, CORES)
    core = peer - chip * CORES
    rank = j * CORES + (core if j % 2 == 0 else CORES - 1 - core)
    return chip * CORES * heads_here + rank


def tile_rows(j, kind, rows):
    return pl.ds(pl.multiple_of((j * KINDS + kind) * rows, rows), rows)


def small_product(left, right):
    return jnp.dot(
        left.astype(jnp.bfloat16), right.astype(jnp.bfloat16), preferred_element_type=jnp.float32
    )


def pair_tables(lists, list_len, live):
    lines, size = lists.shape
    across = lax.broadcasted_iota(jnp.int32, (size, size), 1)
    down = lax.broadcasted_iota(jnp.int32, (size, size), 0)
    lane = lax.broadcasted_iota(jnp.int32, (lines, size), 1)
    line = lax.broadcasted_iota(jnp.int32, (lines, size), 0)
    across_f = across.astype(jnp.float32)
    on_diagonal = (lane >= list_len) & (lane < list_len + 16)
    cell = jnp.where(on_diagonal, (lane - list_len) * 17, lists)
    listed = functools.reduce(lambda x, y: x | y, [(line == j) & (lane < c) for j, c in enumerate(live)])
    row = lax.shift_right_logical(cell, 4).astype(jnp.float32)
    column = jnp.where(on_diagonal | listed, lax.bitwise_and(cell, 15), size).astype(jnp.float32)
    upright = jnp.concatenate([column, row, jnp.zeros((size - 2 * lines, size), jnp.float32)], axis=0).T
    members = [(upright[:, j : j + 1] == across_f).astype(jnp.float32) for j in range(len(live))]
    counted = small_product((across < down).astype(jnp.float32), jnp.concatenate(members, axis=1))
    pairs = [jnp.floor((jnp.sum(member, axis=0, keepdims=True) + 1.0) * 0.5) for member in members]
    pairs_lines = functools.reduce(
        lambda x, y: x + y, [jnp.where(line == j, p, 0.0) for j, p in enumerate(pairs)]
    )
    firsts = small_product(pairs_lines, (down < across).astype(jnp.float32))
    tables = []
    for j, member in enumerate(members):
        earlier = jnp.sum(member * counted[:, j * size : (j + 1) * size], axis=1, keepdims=True)
        half = jnp.floor(earlier * 0.5)
        place = jnp.sum(member * firsts[j : j + 1], axis=1, keepdims=True) + half
        here = jnp.where(place == across_f, jnp.sum(member, axis=1, keepdims=True), 0.0)
        second = earlier - 2.0 * half
        picks = jnp.concatenate([here * (1.0 - second), here * second], axis=1)
        own_column, own_row = column[j : j + 1], row[j : j + 1]
        facts = jnp.where(line == 0, own_column, jnp.where(line == 1, own_row, own_row - NONE))
        found = small_product(facts, picks)
        total = jnp.sum(pairs[j], axis=1, keepdims=True)
        tables.append(
            jnp.where(
                line < 2, found[:, :size], jnp.where(line == 2, found[:, size:] + NONE, total)
            )
        )
    return jnp.concatenate(tables, axis=0)


def tables_kernel(me, counts, order, lists, tables, wide_lists):
    heads_here, list_len = lists.shape
    live = [counts[me[0] * heads_here + j] for j in range(heads_here)]
    wide_lists[...] = jnp.zeros_like(wide_lists)
    wide_lists[:heads_here, :list_len] = lists[...]
    tables[...] = pair_tables(wide_lists[...], list_len, live).astype(jnp.int32)


def share_tables(me, counts, order, lists, peers):
    heads_here = lists.shape[0]
    width = 128
    tables = pl.pallas_call(
        tables_kernel,
        out_shape=jax.ShapeDtypeStruct((heads_here * PAIR_ROWS, width), jnp.int32),
        in_specs=[SMEM, SMEM, SMEM, VMEM],
        out_specs=VMEM,
        scratch_shapes=[pltpu.VMEM((PAIR_ROWS, width), jnp.int32)],
        name="pair_tables",
    )(me, counts, order, lists)
    route = [(s, s ^ 1) for s in range(peers)]
    return jnp.stack([tables, lax.ppermute(tables, "seq", route)])


def pack_kernel(counts, queries, keys, values, packed, order, came, goes, came_sems, goes_sem):
    peers, _, head_dim = packed.shape
    head_total = counts.shape[0]
    rows = queries.shape[0]
    per_chunk = head_total // LOADS
    sources = (queries, keys, values)
    copies = []
    for chunk in range(LOADS):
        span = pl.ds(chunk * per_chunk * head_dim, per_chunk * head_dim)
        for kind, source in enumerate(sources):
            copy = pltpu.make_async_copy(
                source.at[:, span], came.at[kind, :, span], came_sems.at[chunk, kind]
            )
            copy.start()
            copies.append(copy)

    heads_here = head_total // peers
    shared = CORES * heads_here
    weights = [counts[head] * head_total - head for head in range(head_total)]
    ranks = [jnp.int32(0)] * head_total
    for head in range(head_total):
        for other in range(head - head % shared, head):
            ahead = (weights[other] > weights[head]).astype(jnp.int32)
            ranks[head] += ahead
            ranks[other] += 1 - ahead
    for head, rank in enumerate(ranks):
        order[head - head % shared + rank] = head

    for head in range(head_total):
        chunk, first = divmod(head, per_chunk)
        for kind in range(len(sources)):
            if first == 0:
                copies[chunk * len(sources) + kind].wait()
            goes[head, kind * rows : (kind + 1) * rows] = came[
                kind, :, head * head_dim : (head + 1) * head_dim
            ]
        core, j = rank_to_place(ranks[head], heads_here)
        peer = head // shared * CORES + core
        span = pl.ds(pl.multiple_of(j * KINDS * rows, rows), KINDS * rows)
        pltpu.make_async_copy(goes.at[head], packed.at[peer, span], goes_sem).start()
    pltpu.make_async_copy(packed, packed, goes_sem).wait()


def pack(counts, queries, keys, values, peers):
    rows, columns = queries.shape
    head_total = counts.shape[0]
    head_dim = columns // head_total
    heads_here = head_total // peers
    return pl.pallas_call(
        pack_kernel,
        out_shape=(
            jax.ShapeDtypeStruct((peers, heads_here * KINDS * rows, head_dim), queries.dtype),
            jax.ShapeDtypeStruct((head_total,), jnp.int32),
        ),
        in_specs=[SMEM, ANY, ANY, ANY],
        out_specs=(ANY, SMEM),
        scratch_shapes=[
            pltpu.VMEM((KINDS, rows, columns), queries.dtype),
            pltpu.VMEM((head_total, KINDS * rows, head_dim), queries.dtype),
            pltpu.SemaphoreType.DMA((LOADS, KINDS)),
            pltpu.SemaphoreType.DMA,
        ],
        compiler_params=pltpu.CompilerParams(vmem_limit_bytes=60 * 1024 * 1024),
        name="pack",
    )(counts, queries, keys, values)


def unpack_kernel(order, heads, out, staged, sems):
    peers, heads_here, rows, head_dim = heads.shape
    step = rows // CHUNKS
    copies = []
    for chunk in range(CHUNKS):
        span = pl.ds(chunk * step, step)
        for peer in range(peers):
            for j in range(heads_here):
                head = order[place_to_slot(peer, j, heads_here)]
                column = pl.multiple_of(head * head_dim, head_dim)
                staged[span, pl.ds(column, head_dim)] = heads[peer, j, span, :]
        copy = pltpu.make_async_copy(staged.at[span, :], out.at[span, :], sems.at[chunk])
        copy.start()
        copies.append(copy)
    for copy in copies:
        copy.wait()


def unpack(order, heads):
    peers, heads_here, rows, head_dim = heads.shape
    columns = peers * heads_here * head_dim
    return pl.pallas_call(
        unpack_kernel,
        out_shape=jax.ShapeDtypeStruct((rows, columns), heads.dtype),
        in_specs=[SMEM, VMEM],
        out_specs=ANY,
        scratch_shapes=[
            pltpu.VMEM((rows, columns), heads.dtype),
            pltpu.SemaphoreType.DMA((CHUNKS,)),
        ],
        compiler_params=pltpu.CompilerParams(vmem_limit_bytes=8 * 1024 * 1024),
        name="unpack",
    )(order, heads)


def heads_kernel(
    factor, me, order, parcels, all_tables, out, values_t, held, held_max, acc, row_max, row_total, tables, tables_sem
):
    nblocks, heads_here, rows, _ = out.shape
    starts, copies = [], []
    height = all_tables.shape[1]
    for j in range(heads_here):
        head = order[place_to_slot(me[0], j, heads_here)]
        sender = lax.div(head, heads_here)
        copy = pltpu.make_async_copy(
            all_tables.at[lax.bitwise_xor(me[0], sender)],
            tables.at[pl.ds(j * height, height)],
            tables_sem.at[j],
        )
        copy.start()
        copies.append(copy)
        starts.append(j * height + (head - sender * heads_here) * PAIR_ROWS)

    for j in range(heads_here):
        for a in range(nblocks):
            row = j * nblocks + a
            values_t[row] = parcels[a, tile_rows(j, 2, rows), :].T
            acc[row] = jnp.zeros_like(acc[row])
    row_max[...] = jnp.full_like(row_max, -jnp.inf)
    row_total[...] = jnp.zeros_like(row_total)

    for copy in copies:
        copy.wait()
    pairs = [tables[start + 3, 0] for start in starts]
    live = functools.reduce(lambda x, y: x + y, pairs)

    def locate(entry):
        entry = jnp.minimum(entry, live - 1)
        j = jnp.int32(0)
        start, place = starts[0], entry
        for later in range(1, heads_here):
            entry -= pairs[later - 1]
            j = jnp.where(entry >= 0, later, j)
            start = jnp.where(entry >= 0, starts[later], start)
            place = jnp.where(entry >= 0, entry, place)
        b, one, two = (tables[start + line, place] for line in range(3))
        return j, b, one, jnp.where(two == NONE, one, two), two != NONE

    def first_pass(index, carry):
        found = []
        for entry in [index * GROUP + lane for lane in range(GROUP)]:
            j, b, one, two, _ = locate(entry)
            both = jnp.concatenate(
                [parcels[one, tile_rows(j, 0, rows), :], parcels[two, tile_rows(j, 0, rows), :]], axis=0
            )
            scores = factor * lax.dot_general(
                parcels[b, tile_rows(j, 1, rows), :], both, NT, preferred_element_type=jnp.float32
            )
            block_max = jnp.max(scores, axis=0, keepdims=True)
            held[entry] = scores
            held_max[entry] = block_max
            found.append((j * nblocks + one, block_max[:, :rows]))
            found.append((j * nblocks + two, block_max[:, rows:]))
        for row, block_max in found:
            row_max[row] = jnp.maximum(row_max[row], block_max)
        return carry

    steps = (live + GROUP - 1) // GROUP
    lax.fori_loop(0, steps, first_pass, 0)

    def second_pass(index, carry):
        found = []
        for entry in [index * GROUP + lane for lane in range(GROUP)]:
            j, b, one, two, is_two = locate(entry)
            one, two = j * nblocks + one, j * nblocks + two
            block_max = held_max[entry]
            weights = jnp.exp2(held[entry] - block_max)
            is_live = entry < live
            share = jnp.concatenate(
                [
                    jnp.where(is_live, jnp.exp2(block_max[:, :rows] - row_max[one]), 0.0),
                    jnp.where(is_live & is_two, jnp.exp2(block_max[:, rows:] - row_max[two]), 0.0),
                ],
                axis=1,
            )
            total = share * jnp.sum(weights, axis=0, keepdims=True)
            product = share * lax.dot_general(
                values_t[j * nblocks + b],
                weights.astype(jnp.bfloat16),
                NN,
                preferred_element_type=jnp.float32,
            )
            found.append((one, total[:, :rows], product[:, :rows]))
            found.append((two, total[:, rows:], product[:, rows:]))
        for row, total, product in found:
            row_total[row] += total
            acc[row] += product
        return carry

    lax.fori_loop(0, steps, second_pass, 0)

    for j in range(heads_here):
        for a in range(nblocks):
            row = j * nblocks + a
            out[a, j] = (acc[row] * (1.0 / row_total[row])).T.astype(out.dtype)


def attend(me, order, parcels, all_tables, list_len):
    nblocks, parcel_rows, head_dim = parcels.shape
    heads_here = order.shape[0] // nblocks
    rows = parcel_rows // (heads_here * KINDS)
    factor = head_dim ** (-0.5) * math.log2(math.e)
    grid_rows = nblocks * heads_here
    slots = -(-heads_here * (list_len + 2 * nblocks) // (2 * GROUP)) * GROUP
    return pl.pallas_call(
        functools.partial(heads_kernel, factor),
        out_shape=jax.ShapeDtypeStruct((nblocks, heads_here, rows, head_dim), jnp.bfloat16),
        in_specs=[SMEM, SMEM, VMEM, ANY],
        out_specs=VMEM,
        scratch_shapes=[
            pltpu.VMEM((grid_rows, head_dim, rows), jnp.bfloat16),
            pltpu.VMEM((slots, rows, 2 * rows), jnp.float32),
            pltpu.VMEM((slots, 1, 2 * rows), jnp.float32),
            pltpu.VMEM((grid_rows, head_dim, rows), jnp.float32),
            pltpu.VMEM((grid_rows, 1, rows), jnp.float32),
            pltpu.VMEM((grid_rows, 1, rows), jnp.float32),
            pltpu.SMEM((heads_here * all_tables.shape[1], all_tables.shape[2]), jnp.int32),
            pltpu.SemaphoreType.DMA((heads_here,)),
        ],
        compiler_params=pltpu.CompilerParams(vmem_limit_bytes=36 * 1024 * 1024),
        name="attend",
    )(me, order, parcels, all_tables)


def on_device(queries, key_vectors, value_vectors, keep_list, block_counts):
    peers = lax.axis_size("seq")
    me = lax.axis_index("seq").reshape(1)
    packed, order = pack(block_counts, queries, key_vectors, value_vectors, peers)
    parcels = lax.all_to_all(packed, "seq", split_axis=0, concat_axis=0, tiled=True)
    all_tables = share_tables(me, block_counts, order, keep_list, peers)
    attended = attend(me, order, parcels, all_tables, keep_list.shape[1])
    returned = lax.all_to_all(attended, "seq", split_axis=0, concat_axis=0, tiled=True)
    return unpack(order, returned)


def solution(mesh):
    tokens = P(("batch", "seq"), None)
    return jax.shard_map(
        on_device,
        mesh=mesh,
        in_specs=(tokens, tokens, tokens, tokens, P("batch")),
        out_specs=tokens,
        check_vma=False,
    )
```

```python
import functools
import math

import jax
import jax.numpy as jnp
from jax import lax
from jax.experimental import pallas as pl
from jax.experimental.pallas import tpu as pltpu
from jax.sharding import PartitionSpec as P

GROUP = 16
NONE = 16
CHUNKS = 8
LOADS = 4
KINDS = 3
PAIR_ROWS = 8
NT = (((1,), (1,)), ((), ()))
NN = (((1,), (0,)), ((), ()))
VMEM = pl.BlockSpec(memory_space=pltpu.VMEM)
SMEM = pl.BlockSpec(memory_space=pltpu.SMEM)
ANY = pl.BlockSpec(memory_space=pl.ANY)


CORES = 2
ORDER_WIDTH = 128


def rank_to_place(rank, heads_here):
    j = lax.div(rank, CORES)
    core = rank - j * CORES
    return jnp.where(lax.rem(j, 2) == 0, core, CORES - 1 - core), j


def place_to_slot(peer, j, heads_here):
    chip = lax.div(peer, CORES)
    core = peer - chip * CORES
    rank = j * CORES + (core if j % 2 == 0 else CORES - 1 - core)
    return chip * CORES * heads_here + rank


def tile_rows(j, kind, rows):
    return pl.ds(pl.multiple_of((j * KINDS + kind) * rows, rows), rows)


def small_product(left, right):
    return jnp.dot(
        left.astype(jnp.bfloat16), right.astype(jnp.bfloat16), preferred_element_type=jnp.float32
    )


def pair_tables(lists, list_len, live):
    lines, size = lists.shape
    across = lax.broadcasted_iota(jnp.int32, (size, size), 1)
    down = lax.broadcasted_iota(jnp.int32, (size, size), 0)
    lane = lax.broadcasted_iota(jnp.int32, (lines, size), 1)
    line = lax.broadcasted_iota(jnp.int32, (lines, size), 0)
    across_f = across.astype(jnp.float32)
    on_diagonal = (lane >= list_len) & (lane < list_len + 16)
    cell = jnp.where(on_diagonal, (lane - list_len) * 17, lists)
    listed = functools.reduce(lambda x, y: x | y, [(line == j) & (lane < c) for j, c in enumerate(live)])
    row = lax.shift_right_logical(cell, 4).astype(jnp.float32)
    column = jnp.where(on_diagonal | listed, lax.bitwise_and(cell, 15), size).astype(jnp.float32)
    upright = jnp.concatenate([column, row, jnp.zeros((size - 2 * lines, size), jnp.float32)], axis=0).T
    members = [(upright[:, j : j + 1] == across_f).astype(jnp.float32) for j in range(len(live))]
    counted = small_product((across < down).astype(jnp.float32), jnp.concatenate(members, axis=1))
    pairs = [jnp.floor((jnp.sum(member, axis=0, keepdims=True) + 1.0) * 0.5) for member in members]
    pairs_lines = functools.reduce(
        lambda x, y: x + y, [jnp.where(line == j, p, 0.0) for j, p in enumerate(pairs)]
    )
    firsts = small_product(pairs_lines, (down < across).astype(jnp.float32))
    tables = []
    for j, member in enumerate(members):
        earlier = jnp.sum(member * counted[:, j * size : (j + 1) * size], axis=1, keepdims=True)
        half = jnp.floor(earlier * 0.5)
        place = jnp.sum(member * firsts[j : j + 1], axis=1, keepdims=True) + half
        here = jnp.where(place == across_f, jnp.sum(member, axis=1, keepdims=True), 0.0)
        second = earlier - 2.0 * half
        picks = jnp.concatenate([here * (1.0 - second), here * second], axis=1)
        own_column, own_row = column[j : j + 1], row[j : j + 1]
        facts = jnp.where(line == 0, own_column, jnp.where(line == 1, own_row, own_row - NONE))
        found = small_product(facts, picks)
        total = jnp.sum(pairs[j], axis=1, keepdims=True)
        tables.append(
            jnp.where(
                line < 2, found[:, :size], jnp.where(line == 2, found[:, size:] + NONE, total)
            )
        )
    return jnp.concatenate(tables, axis=0)


def tables_kernel(me, counts, order, lists, tables, wide_lists):
    heads_here, list_len = lists.shape
    live = [counts[me[0] * heads_here + j] for j in range(heads_here)]
    wide_lists[...] = jnp.zeros_like(wide_lists)
    wide_lists[:heads_here, :list_len] = lists[...]
    tables[...] = pair_tables(wide_lists[...], list_len, live).astype(jnp.int32)


def own_tables(me, counts, order, lists, peers):
    heads_here = lists.shape[0]
    width = 128
    shape = jax.ShapeDtypeStruct((heads_here * PAIR_ROWS, width), jnp.int32)
    ours = pl.pallas_call(
        tables_kernel,
        out_shape=shape,
        in_specs=[SMEM, SMEM, SMEM, VMEM],
        out_specs=VMEM,
        scratch_shapes=[pltpu.VMEM((PAIR_ROWS, width), jnp.int32)],
        name="pair_tables",
    )(me, counts, order, lists)
    theirs = lax.ppermute(ours, "seq", [(s, s ^ 1) for s in range(peers)])
    tables = jnp.concatenate([ours, theirs]).reshape(CORES * heads_here, PAIR_ROWS, width)
    picked = []
    for j in range(heads_here):
        head = order[0, place_to_slot(me[0], j, heads_here)]
        sender = lax.div(head, heads_here)
        at = head - sender * heads_here + heads_here * (sender != me[0]).astype(jnp.int32)
        picked.append(lax.dynamic_index_in_dim(tables, at, keepdims=False))
    return jnp.concatenate(picked)


def pack_kernel(
    counts, queries, keys, values, packed, order_out, came, goes, order, came_sems, goes_sem, order_sem
):
    peers, _, head_dim = packed.shape
    head_total = counts.shape[0]
    rows = queries.shape[0]
    per_chunk = head_total // LOADS
    sources = (queries, keys, values)
    copies = []
    for chunk in range(LOADS):
        span = pl.ds(chunk * per_chunk * head_dim, per_chunk * head_dim)
        for kind, source in enumerate(sources):
            copy = pltpu.make_async_copy(
                source.at[:, span], came.at[kind, :, span], came_sems.at[chunk, kind]
            )
            copy.start()
            copies.append(copy)

    heads_here = head_total // peers
    shared = CORES * heads_here
    weights = [counts[head] * head_total - head for head in range(head_total)]
    ranks = [jnp.int32(0)] * head_total
    for head in range(head_total):
        for other in range(head - head % shared, head):
            ahead = (weights[other] > weights[head]).astype(jnp.int32)
            ranks[head] += ahead
            ranks[other] += 1 - ahead
    for head, rank in enumerate(ranks):
        order[0, head - head % shared + rank] = head
    order_copy = pltpu.make_async_copy(order, order_out, order_sem)
    order_copy.start()

    for head in range(head_total):
        chunk, first = divmod(head, per_chunk)
        for kind in range(len(sources)):
            if first == 0:
                copies[chunk * len(sources) + kind].wait()
            goes[head, kind * rows : (kind + 1) * rows] = came[
                kind, :, head * head_dim : (head + 1) * head_dim
            ]
        core, j = rank_to_place(ranks[head], heads_here)
        peer = head // shared * CORES + core
        span = pl.ds(pl.multiple_of(j * KINDS * rows, rows), KINDS * rows)
        pltpu.make_async_copy(goes.at[head], packed.at[peer, span], goes_sem).start()
    order_copy.wait()
    pltpu.make_async_copy(packed, packed, goes_sem).wait()


def pack(counts, queries, keys, values, peers):
    rows, columns = queries.shape
    head_total = counts.shape[0]
    head_dim = columns // head_total
    heads_here = head_total // peers
    return pl.pallas_call(
        pack_kernel,
        out_shape=(
            jax.ShapeDtypeStruct((peers, heads_here * KINDS * rows, head_dim), queries.dtype),
            jax.ShapeDtypeStruct((1, ORDER_WIDTH), jnp.int32),
        ),
        in_specs=[SMEM, ANY, ANY, ANY],
        out_specs=(ANY, ANY),
        scratch_shapes=[
            pltpu.VMEM((KINDS, rows, columns), queries.dtype),
            pltpu.VMEM((head_total, KINDS * rows, head_dim), queries.dtype),
            pltpu.SMEM((1, ORDER_WIDTH), jnp.int32),
            pltpu.SemaphoreType.DMA((LOADS, KINDS)),
            pltpu.SemaphoreType.DMA,
            pltpu.SemaphoreType.DMA,
        ],
        compiler_params=pltpu.CompilerParams(vmem_limit_bytes=60 * 1024 * 1024),
        name="pack",
    )(counts, queries, keys, values)


def unpack_kernel(order, heads, out, staged, sems):
    peers, heads_here, rows, head_dim = heads.shape
    step = rows // CHUNKS
    copies = []
    for chunk in range(CHUNKS):
        span = pl.ds(chunk * step, step)
        for peer in range(peers):
            for j in range(heads_here):
                head = order[0, place_to_slot(peer, j, heads_here)]
                column = pl.multiple_of(head * head_dim, head_dim)
                staged[span, pl.ds(column, head_dim)] = heads[peer, j, span, :]
        copy = pltpu.make_async_copy(staged.at[span, :], out.at[span, :], sems.at[chunk])
        copy.start()
        copies.append(copy)
    for copy in copies:
        copy.wait()


def unpack(order, heads):
    peers, heads_here, rows, head_dim = heads.shape
    columns = peers * heads_here * head_dim
    return pl.pallas_call(
        unpack_kernel,
        out_shape=jax.ShapeDtypeStruct((rows, columns), heads.dtype),
        in_specs=[SMEM, VMEM],
        out_specs=ANY,
        scratch_shapes=[
            pltpu.VMEM((rows, columns), heads.dtype),
            pltpu.SemaphoreType.DMA((CHUNKS,)),
        ],
        compiler_params=pltpu.CompilerParams(vmem_limit_bytes=8 * 1024 * 1024),
        name="unpack",
    )(order, heads)


def heads_kernel(factor, tables_in, parcels, out, values_t, held, held_max, tables, tables_sem, acc, row_max, row_total):
    nblocks, heads_here, rows, _ = out.shape
    starts = [j * PAIR_ROWS for j in range(heads_here)]
    tables_copy = pltpu.make_async_copy(tables_in, tables, tables_sem)
    tables_copy.start()
    for j in range(heads_here):
        for a in range(nblocks):
            row = j * nblocks + a
            values_t[row] = parcels[a, tile_rows(j, 2, rows), :].T
            acc[row] = jnp.zeros_like(acc[row])
    row_max[...] = jnp.full_like(row_max, -jnp.inf)
    row_total[...] = jnp.zeros_like(row_total)

    tables_copy.wait()
    pairs = [tables[start + 3, 0] for start in starts]
    live = functools.reduce(lambda x, y: x + y, pairs)

    def locate(entry):
        entry = jnp.minimum(entry, live - 1)
        j = jnp.int32(0)
        start, place = starts[0], entry
        for later in range(1, heads_here):
            entry -= pairs[later - 1]
            j = jnp.where(entry >= 0, later, j)
            start = jnp.where(entry >= 0, starts[later], start)
            place = jnp.where(entry >= 0, entry, place)
        b, one, two = (tables[start + line, place] for line in range(3))
        return j, b, one, jnp.where(two == NONE, one, two), two != NONE

    def first_pass(index, carry):
        found = []
        for entry in [index * GROUP + lane for lane in range(GROUP)]:
            j, b, one, two, _ = locate(entry)
            both = jnp.concatenate(
                [parcels[one, tile_rows(j, 0, rows), :], parcels[two, tile_rows(j, 0, rows), :]], axis=0
            )
            scores = factor * lax.dot_general(
                parcels[b, tile_rows(j, 1, rows), :], both, NT, preferred_element_type=jnp.float32
            )
            block_max = jnp.max(scores, axis=0, keepdims=True)
            held[entry] = scores
            held_max[entry] = block_max
            found.append((j * nblocks + one, block_max[:, :rows]))
            found.append((j * nblocks + two, block_max[:, rows:]))
        for row, block_max in found:
            row_max[row] = jnp.maximum(row_max[row], block_max)
        return carry

    steps = (live + GROUP - 1) // GROUP
    lax.fori_loop(0, steps, first_pass, 0)

    def second_pass(index, carry):
        found = []
        for entry in [index * GROUP + lane for lane in range(GROUP)]:
            j, b, one, two, is_two = locate(entry)
            one, two = j * nblocks + one, j * nblocks + two
            block_max = held_max[entry]
            weights = jnp.exp2(held[entry] - block_max)
            is_live = entry < live
            share = jnp.concatenate(
                [
                    jnp.where(is_live, jnp.exp2(block_max[:, :rows] - row_max[one]), 0.0),
                    jnp.where(is_live & is_two, jnp.exp2(block_max[:, rows:] - row_max[two]), 0.0),
                ],
                axis=1,
            )
            total = share * jnp.sum(weights, axis=0, keepdims=True)
            product = share * lax.dot_general(
                values_t[j * nblocks + b],
                weights.astype(jnp.bfloat16),
                NN,
                preferred_element_type=jnp.float32,
            )
            found.append((one, total[:, :rows], product[:, :rows]))
            found.append((two, total[:, rows:], product[:, rows:]))
        for row, total, product in found:
            row_total[row] += total
            acc[row] += product
        return carry

    lax.fori_loop(0, steps, second_pass, 0)

    for j in range(heads_here):
        for a in range(nblocks):
            row = j * nblocks + a
            out[a, j] = (acc[row] * (1.0 / row_total[row])).T.astype(out.dtype)


def attend(tables, parcels, list_len):
    nblocks, parcel_rows, head_dim = parcels.shape
    heads_here = tables.shape[0] // PAIR_ROWS
    rows = parcel_rows // (heads_here * KINDS)
    factor = head_dim ** (-0.5) * math.log2(math.e)
    grid_rows = nblocks * heads_here
    slots = -(-heads_here * (list_len + 2 * nblocks) // (2 * GROUP)) * GROUP
    return pl.pallas_call(
        functools.partial(heads_kernel, factor),
        out_shape=jax.ShapeDtypeStruct((nblocks, heads_here, rows, head_dim), jnp.bfloat16),
        in_specs=[ANY, VMEM],
        out_specs=VMEM,
        scratch_shapes=[
            pltpu.VMEM((grid_rows, head_dim, rows), jnp.bfloat16),
            pltpu.VMEM((slots, rows, 2 * rows), jnp.float32),
            pltpu.VMEM((slots, 1, 2 * rows), jnp.float32),
            pltpu.SMEM(tables.shape, jnp.int32),
            pltpu.SemaphoreType.DMA,
            pltpu.VMEM((grid_rows, head_dim, rows), jnp.float32),
            pltpu.VMEM((grid_rows, 1, rows), jnp.float32),
            pltpu.VMEM((grid_rows, 1, rows), jnp.float32),
        ],
        compiler_params=pltpu.CompilerParams(vmem_limit_bytes=36 * 1024 * 1024),
        name="attend",
    )(tables, parcels)


def on_device(queries, key_vectors, value_vectors, keep_list, block_counts):
    peers = lax.axis_size("seq")
    me = lax.axis_index("seq").reshape(1)
    packed, order = pack(block_counts, queries, key_vectors, value_vectors, peers)
    parcels = lax.all_to_all(packed, "seq", split_axis=0, concat_axis=0, tiled=True)
    tables = own_tables(me, block_counts, order, keep_list, peers)
    attended = attend(tables, parcels, keep_list.shape[1])
    returned = lax.all_to_all(attended, "seq", split_axis=0, concat_axis=0, tiled=True)
    return unpack(order, returned)


def solution(mesh):
    tokens = P(("batch", "seq"), None)
    return jax.shard_map(
        on_device,
        mesh=mesh,
        in_specs=(tokens, tokens, tokens, tokens, P("batch")),
        out_specs=tokens,
        check_vma=False,
    )
```

```python
import functools
import math

import jax
import jax.numpy as jnp
from jax import lax
from jax.experimental import pallas as pl
from jax.experimental.pallas import tpu as pltpu
from jax.sharding import PartitionSpec as P

GROUP = 16
NONE = 16
CHUNKS = 8
LOADS = 4
KINDS = 3
PAIR_ROWS = 8
NT = (((1,), (1,)), ((), ()))
NN = (((1,), (0,)), ((), ()))
VMEM = pl.BlockSpec(memory_space=pltpu.VMEM)
SMEM = pl.BlockSpec(memory_space=pltpu.SMEM)
ANY = pl.BlockSpec(memory_space=pl.ANY)


CORES = 2
ORDER_WIDTH = 128


def rank_to_place(rank, heads_here):
    j = lax.div(rank, CORES)
    core = rank - j * CORES
    return jnp.where(lax.rem(j, 2) == 0, core, CORES - 1 - core), j


def place_to_slot(peer, j, heads_here):
    chip = lax.div(peer, CORES)
    core = peer - chip * CORES
    rank = j * CORES + (core if j % 2 == 0 else CORES - 1 - core)
    return chip * CORES * heads_here + rank


def tile_rows(j, kind, rows):
    return pl.ds(pl.multiple_of((j * KINDS + kind) * rows, rows), rows)


def small_product(left, right):
    return jnp.dot(
        left.astype(jnp.bfloat16), right.astype(jnp.bfloat16), preferred_element_type=jnp.float32
    )


def pair_tables(lists, list_len, live):
    lines, size = lists.shape
    across = lax.broadcasted_iota(jnp.int32, (size, size), 1)
    down = lax.broadcasted_iota(jnp.int32, (size, size), 0)
    lane = lax.broadcasted_iota(jnp.int32, (lines, size), 1)
    line = lax.broadcasted_iota(jnp.int32, (lines, size), 0)
    across_f = across.astype(jnp.float32)
    on_diagonal = (lane >= list_len) & (lane < list_len + 16)
    cell = jnp.where(on_diagonal, (lane - list_len) * 17, lists)
    listed = functools.reduce(lambda x, y: x | y, [(line == j) & (lane < c) for j, c in enumerate(live)])
    row = lax.shift_right_logical(cell, 4).astype(jnp.float32)
    column = jnp.where(on_diagonal | listed, lax.bitwise_and(cell, 15), size).astype(jnp.float32)
    upright = jnp.concatenate([column, row, jnp.zeros((size - 2 * lines, size), jnp.float32)], axis=0).T
    members = [(upright[:, j : j + 1] == across_f).astype(jnp.float32) for j in range(len(live))]
    counted = small_product((across < down).astype(jnp.float32), jnp.concatenate(members, axis=1))
    pairs = [jnp.floor((jnp.sum(member, axis=0, keepdims=True) + 1.0) * 0.5) for member in members]
    pairs_lines = functools.reduce(
        lambda x, y: x + y, [jnp.where(line == j, p, 0.0) for j, p in enumerate(pairs)]
    )
    firsts = small_product(pairs_lines, (down < across).astype(jnp.float32))
    tables = []
    for j, member in enumerate(members):
        earlier = jnp.sum(member * counted[:, j * size : (j + 1) * size], axis=1, keepdims=True)
        half = jnp.floor(earlier * 0.5)
        place = jnp.sum(member * firsts[j : j + 1], axis=1, keepdims=True) + half
        here = jnp.where(place == across_f, jnp.sum(member, axis=1, keepdims=True), 0.0)
        second = earlier - 2.0 * half
        picks = jnp.concatenate([here * (1.0 - second), here * second], axis=1)
        own_column, own_row = column[j : j + 1], row[j : j + 1]
        facts = jnp.where(line == 0, own_column, jnp.where(line == 1, own_row, own_row - NONE))
        found = small_product(facts, picks)
        total = jnp.sum(pairs[j], axis=1, keepdims=True)
        tables.append(
            jnp.where(
                line < 2, found[:, :size], jnp.where(line == 2, found[:, size:] + NONE, total)
            )
        )
    return jnp.concatenate(tables, axis=0)


def tables_kernel(me, counts, order, lists, tables, wide_lists):
    heads_here, list_len = lists.shape
    live = [counts[me[0] * heads_here + j] for j in range(heads_here)]
    wide_lists[...] = jnp.zeros_like(wide_lists)
    wide_lists[:heads_here, :list_len] = lists[...]
    tables[...] = pair_tables(wide_lists[...], list_len, live).astype(jnp.int32)


def own_tables(me, counts, order, lists, peers):
    heads_here = lists.shape[0]
    width = 128
    shape = jax.ShapeDtypeStruct((heads_here * PAIR_ROWS, width), jnp.int32)
    ours = pl.pallas_call(
        tables_kernel,
        out_shape=shape,
        in_specs=[SMEM, SMEM, SMEM, VMEM],
        out_specs=VMEM,
        scratch_shapes=[pltpu.VMEM((PAIR_ROWS, width), jnp.int32)],
        name="pair_tables",
    )(me, counts, order, lists)
    theirs = lax.ppermute(ours, "seq", [(s, s ^ 1) for s in range(peers)])
    tables = jnp.concatenate([ours, theirs]).reshape(CORES * heads_here, PAIR_ROWS, width)
    picked = []
    for j in range(heads_here):
        head = order[0, place_to_slot(me[0], j, heads_here)]
        sender = lax.div(head, heads_here)
        at = head - sender * heads_here + heads_here * (sender != me[0]).astype(jnp.int32)
        picked.append(lax.dynamic_index_in_dim(tables, at, keepdims=False))
    return jnp.concatenate(picked)


def pack_kernel(
    counts_in, queries, keys, values, packed, order_out, came, goes, counts, order, came_sems, goes_sem, small_sems
):
    peers, _, head_dim = packed.shape
    head_total = counts.shape[0]
    rows = queries.shape[0]
    per_chunk = head_total // LOADS
    sources = (queries, keys, values)
    counts_copy = pltpu.make_async_copy(counts_in, counts, small_sems.at[0])
    counts_copy.start()
    copies = []
    for chunk in range(LOADS):
        span = pl.ds(chunk * per_chunk * head_dim, per_chunk * head_dim)
        for kind, source in enumerate(sources):
            copy = pltpu.make_async_copy(
                source.at[:, span], came.at[kind, :, span], came_sems.at[chunk, kind]
            )
            copy.start()
            copies.append(copy)

    heads_here = head_total // peers
    shared = CORES * heads_here
    counts_copy.wait()
    weights = [counts[head] * head_total - head for head in range(head_total)]
    ranks = [jnp.int32(0)] * head_total
    for head in range(head_total):
        for other in range(head - head % shared, head):
            ahead = (weights[other] > weights[head]).astype(jnp.int32)
            ranks[head] += ahead
            ranks[other] += 1 - ahead
    for head, rank in enumerate(ranks):
        order[0, head - head % shared + rank] = head
    order_copy = pltpu.make_async_copy(order, order_out, small_sems.at[1])
    order_copy.start()

    for head in range(head_total):
        chunk, first = divmod(head, per_chunk)
        for kind in range(len(sources)):
            if first == 0:
                copies[chunk * len(sources) + kind].wait()
            goes[head, kind * rows : (kind + 1) * rows] = came[
                kind, :, head * head_dim : (head + 1) * head_dim
            ]
        core, j = rank_to_place(ranks[head], heads_here)
        peer = head // shared * CORES + core
        span = pl.ds(pl.multiple_of(j * KINDS * rows, rows), KINDS * rows)
        pltpu.make_async_copy(goes.at[head], packed.at[peer, span], goes_sem).start()
    order_copy.wait()
    pltpu.make_async_copy(packed, packed, goes_sem).wait()


def pack(counts, queries, keys, values, peers):
    rows, columns = queries.shape
    head_total = counts.shape[0]
    head_dim = columns // head_total
    heads_here = head_total // peers
    return pl.pallas_call(
        pack_kernel,
        out_shape=(
            jax.ShapeDtypeStruct((peers, heads_here * KINDS * rows, head_dim), queries.dtype),
            jax.ShapeDtypeStruct((1, ORDER_WIDTH), jnp.int32),
        ),
        in_specs=[ANY, ANY, ANY, ANY],
        out_specs=(ANY, ANY),
        scratch_shapes=[
            pltpu.VMEM((KINDS, rows, columns), queries.dtype),
            pltpu.VMEM((head_total, KINDS * rows, head_dim), queries.dtype),
            pltpu.SMEM((head_total,), jnp.int32),
            pltpu.SMEM((1, ORDER_WIDTH), jnp.int32),
            pltpu.SemaphoreType.DMA((LOADS, KINDS)),
            pltpu.SemaphoreType.DMA,
            pltpu.SemaphoreType.DMA((2,)),
        ],
        compiler_params=pltpu.CompilerParams(vmem_limit_bytes=60 * 1024 * 1024),
        name="pack",
    )(counts, queries, keys, values)


def unpack_kernel(order, heads, out, staged, sems):
    peers, heads_here, rows, head_dim = heads.shape
    step = rows // CHUNKS
    copies = []
    for chunk in range(CHUNKS):
        span = pl.ds(chunk * step, step)
        for peer in range(peers):
            for j in range(heads_here):
                head = order[0, place_to_slot(peer, j, heads_here)]
                column = pl.multiple_of(head * head_dim, head_dim)
                staged[span, pl.ds(column, head_dim)] = heads[peer, j, span, :]
        copy = pltpu.make_async_copy(staged.at[span, :], out.at[span, :], sems.at[chunk])
        copy.start()
        copies.append(copy)
    for copy in copies:
        copy.wait()


def unpack(order, heads):
    peers, heads_here, rows, head_dim = heads.shape
    columns = peers * heads_here * head_dim
    return pl.pallas_call(
        unpack_kernel,
        out_shape=jax.ShapeDtypeStruct((rows, columns), heads.dtype),
        in_specs=[SMEM, VMEM],
        out_specs=ANY,
        scratch_shapes=[
            pltpu.VMEM((rows, columns), heads.dtype),
            pltpu.SemaphoreType.DMA((CHUNKS,)),
        ],
        compiler_params=pltpu.CompilerParams(vmem_limit_bytes=8 * 1024 * 1024),
        name="unpack",
    )(order, heads)


def heads_kernel(factor, tables_in, parcels, out, values_t, held, held_max, tables, tables_sem, acc, row_max, row_total):
    nblocks, heads_here, rows, _ = out.shape
    starts = [j * PAIR_ROWS for j in range(heads_here)]
    tables_copy = pltpu.make_async_copy(tables_in, tables, tables_sem)
    tables_copy.start()
    for j in range(heads_here):
        for a in range(nblocks):
            row = j * nblocks + a
            values_t[row] = parcels[a, tile_rows(j, 2, rows), :].T
            acc[row] = jnp.zeros_like(acc[row])
    row_max[...] = jnp.full_like(row_max, -jnp.inf)
    row_total[...] = jnp.zeros_like(row_total)

    tables_copy.wait()
    pairs = [tables[start + 3, 0] for start in starts]
    live = functools.reduce(lambda x, y: x + y, pairs)

    def locate(entry):
        entry = jnp.minimum(entry, live - 1)
        j = jnp.int32(0)
        start, place = starts[0], entry
        for later in range(1, heads_here):
            entry -= pairs[later - 1]
            j = jnp.where(entry >= 0, later, j)
            start = jnp.where(entry >= 0, starts[later], start)
            place = jnp.where(entry >= 0, entry, place)
        b, one, two = (tables[start + line, place] for line in range(3))
        return j, b, one, jnp.where(two == NONE, one, two), two != NONE

    def first_pass(index, carry):
        found = []
        for entry in [index * GROUP + lane for lane in range(GROUP)]:
            j, b, one, two, _ = locate(entry)
            both = jnp.concatenate(
                [parcels[one, tile_rows(j, 0, rows), :], parcels[two, tile_rows(j, 0, rows), :]], axis=0
            )
            scores = factor * lax.dot_general(
                parcels[b, tile_rows(j, 1, rows), :], both, NT, preferred_element_type=jnp.float32
            )
            block_max = jnp.max(scores, axis=0, keepdims=True)
            held[entry] = scores
            held_max[entry] = block_max
            found.append((j * nblocks + one, block_max[:, :rows]))
            found.append((j * nblocks + two, block_max[:, rows:]))
        for row, block_max in found:
            row_max[row] = jnp.maximum(row_max[row], block_max)
        return carry

    steps = (live + GROUP - 1) // GROUP
    lax.fori_loop(0, steps, first_pass, 0)

    def second_pass(index, carry):
        found = []
        for entry in [index * GROUP + lane for lane in range(GROUP)]:
            j, b, one, two, is_two = locate(entry)
            one, two = j * nblocks + one, j * nblocks + two
            block_max = held_max[entry]
            weights = jnp.exp2(held[entry] - block_max)
            is_live = entry < live
            share = jnp.concatenate(
                [
                    jnp.where(is_live, jnp.exp2(block_max[:, :rows] - row_max[one]), 0.0),
                    jnp.where(is_live & is_two, jnp.exp2(block_max[:, rows:] - row_max[two]), 0.0),
                ],
                axis=1,
            )
            total = share * jnp.sum(weights, axis=0, keepdims=True)
            product = share * lax.dot_general(
                values_t[j * nblocks + b],
                weights.astype(jnp.bfloat16),
                NN,
                preferred_element_type=jnp.float32,
            )
            found.append((one, total[:, :rows], product[:, :rows]))
            found.append((two, total[:, rows:], product[:, rows:]))
        for row, total, product in found:
            row_total[row] += total
            acc[row] += product
        return carry

    lax.fori_loop(0, steps, second_pass, 0)

    for j in range(heads_here):
        for a in range(nblocks):
            row = j * nblocks + a
            out[a, j] = (acc[row] * (1.0 / row_total[row])).T.astype(out.dtype)


def attend(tables, parcels, list_len):
    nblocks, parcel_rows, head_dim = parcels.shape
    heads_here = tables.shape[0] // PAIR_ROWS
    rows = parcel_rows // (heads_here * KINDS)
    factor = head_dim ** (-0.5) * math.log2(math.e)
    grid_rows = nblocks * heads_here
    slots = -(-heads_here * (list_len + 2 * nblocks) // (2 * GROUP)) * GROUP
    return pl.pallas_call(
        functools.partial(heads_kernel, factor),
        out_shape=jax.ShapeDtypeStruct((nblocks, heads_here, rows, head_dim), jnp.bfloat16),
        in_specs=[ANY, VMEM],
        out_specs=VMEM,
        scratch_shapes=[
            pltpu.VMEM((grid_rows, head_dim, rows), jnp.bfloat16),
            pltpu.VMEM((slots, rows, 2 * rows), jnp.float32),
            pltpu.VMEM((slots, 1, 2 * rows), jnp.float32),
            pltpu.SMEM(tables.shape, jnp.int32),
            pltpu.SemaphoreType.DMA,
            pltpu.VMEM((grid_rows, head_dim, rows), jnp.float32),
            pltpu.VMEM((grid_rows, 1, rows), jnp.float32),
            pltpu.VMEM((grid_rows, 1, rows), jnp.float32),
        ],
        compiler_params=pltpu.CompilerParams(vmem_limit_bytes=36 * 1024 * 1024),
        name="attend",
    )(tables, parcels)


def on_device(queries, key_vectors, value_vectors, keep_list, block_counts):
    peers = lax.axis_size("seq")
    me = lax.axis_index("seq").reshape(1)
    packed, order = pack(block_counts, queries, key_vectors, value_vectors, peers)
    parcels = lax.all_to_all(packed, "seq", split_axis=0, concat_axis=0, tiled=True)
    tables = own_tables(me, block_counts, order, keep_list, peers)
    attended = attend(tables, parcels, keep_list.shape[1])
    returned = lax.all_to_all(attended, "seq", split_axis=0, concat_axis=0, tiled=True)
    return unpack(order, returned)


def solution(mesh):
    tokens = P(("batch", "seq"), None)
    return jax.shard_map(
        on_device,
        mesh=mesh,
        in_specs=(tokens, tokens, tokens, tokens, P("batch")),
        out_specs=tokens,
        check_vma=False,
    )
```

```python
import functools
import math

import jax
import jax.numpy as jnp
from jax import lax
from jax.experimental import pallas as pl
from jax.experimental.pallas import tpu as pltpu
from jax.sharding import PartitionSpec as P

GROUP = 16
NONE = 16
LOADS = 4
KINDS = 3
PAIR_ROWS = 8
NT = (((1,), (1,)), ((), ()))
NN = (((1,), (0,)), ((), ()))
VMEM = pl.BlockSpec(memory_space=pltpu.VMEM)
SMEM = pl.BlockSpec(memory_space=pltpu.SMEM)
ANY = pl.BlockSpec(memory_space=pl.ANY)


CORES = 2
ORDER_WIDTH = 128


def rank_to_place(rank, heads_here):
    j = lax.div(rank, CORES)
    core = rank - j * CORES
    return jnp.where(lax.rem(j, 2) == 0, core, CORES - 1 - core), j


def place_to_slot(peer, j, heads_here):
    chip = lax.div(peer, CORES)
    core = peer - chip * CORES
    rank = j * CORES + (core if j % 2 == 0 else CORES - 1 - core)
    return chip * CORES * heads_here + rank


def tile_rows(j, kind, rows):
    return pl.ds(pl.multiple_of((j * KINDS + kind) * rows, rows), rows)


def small_product(left, right):
    return jnp.dot(
        left.astype(jnp.bfloat16), right.astype(jnp.bfloat16), preferred_element_type=jnp.float32
    )


def pair_tables(lists, list_len, live):
    lines, size = lists.shape
    across = lax.broadcasted_iota(jnp.int32, (size, size), 1)
    down = lax.broadcasted_iota(jnp.int32, (size, size), 0)
    lane = lax.broadcasted_iota(jnp.int32, (lines, size), 1)
    line = lax.broadcasted_iota(jnp.int32, (lines, size), 0)
    across_f = across.astype(jnp.float32)
    on_diagonal = (lane >= list_len) & (lane < list_len + 16)
    cell = jnp.where(on_diagonal, (lane - list_len) * 17, lists)
    listed = functools.reduce(lambda x, y: x | y, [(line == j) & (lane < c) for j, c in enumerate(live)])
    row = lax.shift_right_logical(cell, 4).astype(jnp.float32)
    column = jnp.where(on_diagonal | listed, lax.bitwise_and(cell, 15), size).astype(jnp.float32)
    upright = jnp.concatenate([column, row, jnp.zeros((size - 2 * lines, size), jnp.float32)], axis=0).T
    members = [(upright[:, j : j + 1] == across_f).astype(jnp.float32) for j in range(len(live))]
    counted = small_product((across < down).astype(jnp.float32), jnp.concatenate(members, axis=1))
    pairs = [jnp.floor((jnp.sum(member, axis=0, keepdims=True) + 1.0) * 0.5) for member in members]
    pairs_lines = functools.reduce(
        lambda x, y: x + y, [jnp.where(line == j, p, 0.0) for j, p in enumerate(pairs)]
    )
    firsts = small_product(pairs_lines, (down < across).astype(jnp.float32))
    tables = []
    for j, member in enumerate(members):
        earlier = jnp.sum(member * counted[:, j * size : (j + 1) * size], axis=1, keepdims=True)
        half = jnp.floor(earlier * 0.5)
        place = jnp.sum(member * firsts[j : j + 1], axis=1, keepdims=True) + half
        here = jnp.where(place == across_f, jnp.sum(member, axis=1, keepdims=True), 0.0)
        second = earlier - 2.0 * half
        picks = jnp.concatenate([here * (1.0 - second), here * second], axis=1)
        own_column, own_row = column[j : j + 1], row[j : j + 1]
        facts = jnp.where(line == 0, own_column, jnp.where(line == 1, own_row, own_row - NONE))
        found = small_product(facts, picks)
        total = jnp.sum(pairs[j], axis=1, keepdims=True)
        tables.append(
            jnp.where(
                line < 2, found[:, :size], jnp.where(line == 2, found[:, size:] + NONE, total)
            )
        )
    return jnp.concatenate(tables, axis=0)


def tables_kernel(me, counts, order, lists, tables, wide_lists):
    heads_here, list_len = lists.shape
    live = [counts[me[0] * heads_here + j] for j in range(heads_here)]
    wide_lists[...] = jnp.zeros_like(wide_lists)
    wide_lists[:heads_here, :list_len] = lists[...]
    tables[...] = pair_tables(wide_lists[...], list_len, live).astype(jnp.int32)


def own_tables(me, counts, order, lists, peers):
    heads_here = lists.shape[0]
    width = 128
    shape = jax.ShapeDtypeStruct((heads_here * PAIR_ROWS, width), jnp.int32)
    ours = pl.pallas_call(
        tables_kernel,
        out_shape=shape,
        in_specs=[SMEM, SMEM, SMEM, VMEM],
        out_specs=VMEM,
        scratch_shapes=[pltpu.VMEM((PAIR_ROWS, width), jnp.int32)],
        name="pair_tables",
    )(me, counts, order, lists)
    theirs = lax.ppermute(ours, "seq", [(s, s ^ 1) for s in range(peers)])
    tables = jnp.concatenate([ours, theirs]).reshape(CORES * heads_here, PAIR_ROWS, width)
    picked = []
    for j in range(heads_here):
        head = order[0, place_to_slot(me[0], j, heads_here)]
        sender = lax.div(head, heads_here)
        at = head - sender * heads_here + heads_here * (sender != me[0]).astype(jnp.int32)
        picked.append(lax.dynamic_index_in_dim(tables, at, keepdims=False))
    return jnp.concatenate(picked)


def pack_kernel(
    counts_in, queries, keys, values, packed, order_out, came, goes, counts, order, came_sems, goes_sem, small_sems
):
    peers, _, head_dim = packed.shape
    head_total = counts.shape[0]
    rows = queries.shape[0]
    per_chunk = head_total // LOADS
    sources = (queries, keys, values)
    counts_copy = pltpu.make_async_copy(counts_in, counts, small_sems.at[0])
    counts_copy.start()
    copies = []
    for chunk in range(LOADS):
        span = pl.ds(chunk * per_chunk * head_dim, per_chunk * head_dim)
        for kind, source in enumerate(sources):
            copy = pltpu.make_async_copy(
                source.at[:, span], came.at[kind, :, span], came_sems.at[chunk, kind]
            )
            copy.start()
            copies.append(copy)

    heads_here = head_total // peers
    shared = CORES * heads_here
    counts_copy.wait()
    weights = [counts[head] * head_total - head for head in range(head_total)]
    ranks = [jnp.int32(0)] * head_total
    for head in range(head_total):
        for other in range(head - head % shared, head):
            ahead = (weights[other] > weights[head]).astype(jnp.int32)
            ranks[head] += ahead
            ranks[other] += 1 - ahead
    for head, rank in enumerate(ranks):
        order[0, head - head % shared + rank] = head
    order_copy = pltpu.make_async_copy(order, order_out, small_sems.at[1])
    order_copy.start()

    for head in range(head_total):
        chunk, first = divmod(head, per_chunk)
        for kind in range(len(sources)):
            if first == 0:
                copies[chunk * len(sources) + kind].wait()
            goes[head, kind * rows : (kind + 1) * rows] = came[
                kind, :, head * head_dim : (head + 1) * head_dim
            ]
        core, j = rank_to_place(ranks[head], heads_here)
        peer = head // shared * CORES + core
        span = pl.ds(pl.multiple_of(j * KINDS * rows, rows), KINDS * rows)
        pltpu.make_async_copy(goes.at[head], packed.at[peer, span], goes_sem).start()
    order_copy.wait()
    pltpu.make_async_copy(packed, packed, goes_sem).wait()


def pack(counts, queries, keys, values, peers):
    rows, columns = queries.shape
    head_total = counts.shape[0]
    head_dim = columns // head_total
    heads_here = head_total // peers
    return pl.pallas_call(
        pack_kernel,
        out_shape=(
            jax.ShapeDtypeStruct((peers, heads_here * KINDS * rows, head_dim), queries.dtype),
            jax.ShapeDtypeStruct((1, ORDER_WIDTH), jnp.int32),
        ),
        in_specs=[ANY, ANY, ANY, ANY],
        out_specs=(ANY, ANY),
        scratch_shapes=[
            pltpu.VMEM((KINDS, rows, columns), queries.dtype),
            pltpu.VMEM((head_total, KINDS * rows, head_dim), queries.dtype),
            pltpu.SMEM((head_total,), jnp.int32),
            pltpu.SMEM((1, ORDER_WIDTH), jnp.int32),
            pltpu.SemaphoreType.DMA((LOADS, KINDS)),
            pltpu.SemaphoreType.DMA,
            pltpu.SemaphoreType.DMA((2,)),
        ],
        compiler_params=pltpu.CompilerParams(vmem_limit_bytes=60 * 1024 * 1024),
        name="pack",
    )(counts, queries, keys, values)


def static_slot(peer, j, heads_here):
    chip, core = divmod(peer, CORES)
    return chip * CORES * heads_here + j * CORES + (core if j % 2 == 0 else CORES - 1 - core)


def unpack_kernel(order, heads, out, sem):
    peers, heads_here, _, head_dim = heads.shape
    held_order = order[...]
    for peer in range(peers):
        for j in range(heads_here):
            slot = static_slot(peer, j, heads_here)
            head = held_order[0, slot]
            column = pl.multiple_of(head * head_dim, head_dim)
            pltpu.make_async_copy(heads.at[peer, j], out.at[:, pl.ds(column, head_dim)], sem).start()
    pltpu.make_async_copy(out, out, sem).wait()


def unpack(order, heads):
    peers, heads_here, rows, head_dim = heads.shape
    columns = peers * heads_here * head_dim
    return pl.pallas_call(
        unpack_kernel,
        out_shape=jax.ShapeDtypeStruct((rows, columns), heads.dtype),
        in_specs=[VMEM, VMEM],
        out_specs=ANY,
        scratch_shapes=[
            pltpu.SemaphoreType.DMA,
        ],
        compiler_params=pltpu.CompilerParams(vmem_limit_bytes=8 * 1024 * 1024),
        name="unpack",
    )(order, heads)


def heads_kernel(factor, tables_in, parcels, out, values_t, held, held_max, tables, tables_sem, acc, row_max, row_total):
    nblocks, heads_here, rows, _ = out.shape
    starts = [j * PAIR_ROWS for j in range(heads_here)]
    tables_copy = pltpu.make_async_copy(tables_in, tables, tables_sem)
    tables_copy.start()
    for j in range(heads_here):
        for a in range(nblocks):
            row = j * nblocks + a
            values_t[row] = parcels[a, tile_rows(j, 2, rows), :].T
            acc[row] = jnp.zeros_like(acc[row])
    row_max[...] = jnp.full_like(row_max, -jnp.inf)
    row_total[...] = jnp.zeros_like(row_total)

    tables_copy.wait()
    pairs = [tables[start + 3, 0] for start in starts]
    live = functools.reduce(lambda x, y: x + y, pairs)

    def locate(entry):
        entry = jnp.minimum(entry, live - 1)
        j = jnp.int32(0)
        start, place = starts[0], entry
        for later in range(1, heads_here):
            entry -= pairs[later - 1]
            j = jnp.where(entry >= 0, later, j)
            start = jnp.where(entry >= 0, starts[later], start)
            place = jnp.where(entry >= 0, entry, place)
        b, one, two = (tables[start + line, place] for line in range(3))
        return j, b, one, jnp.where(two == NONE, one, two), two != NONE

    def first_pass(index, carry):
        found = []
        for entry in [index * GROUP + lane for lane in range(GROUP)]:
            j, b, one, two, _ = locate(entry)
            both = jnp.concatenate(
                [parcels[one, tile_rows(j, 0, rows), :], parcels[two, tile_rows(j, 0, rows), :]], axis=0
            )
            scores = factor * lax.dot_general(
                parcels[b, tile_rows(j, 1, rows), :], both, NT, preferred_element_type=jnp.float32
            )
            block_max = jnp.max(scores, axis=0, keepdims=True)
            held[entry] = scores
            held_max[entry] = block_max
            found.append((j * nblocks + one, block_max[:, :rows]))
            found.append((j * nblocks + two, block_max[:, rows:]))
        for row, block_max in found:
            row_max[row] = jnp.maximum(row_max[row], block_max)
        return carry

    steps = (live + GROUP - 1) // GROUP
    lax.fori_loop(0, steps, first_pass, 0)

    def second_pass(index, carry):
        found = []
        for entry in [index * GROUP + lane for lane in range(GROUP)]:
            j, b, one, two, is_two = locate(entry)
            one, two = j * nblocks + one, j * nblocks + two
            block_max = held_max[entry]
            weights = jnp.exp2(held[entry] - block_max)
            is_live = entry < live
            share = jnp.concatenate(
                [
                    jnp.where(is_live, jnp.exp2(block_max[:, :rows] - row_max[one]), 0.0),
                    jnp.where(is_live & is_two, jnp.exp2(block_max[:, rows:] - row_max[two]), 0.0),
                ],
                axis=1,
            )
            total = share * jnp.sum(weights, axis=0, keepdims=True)
            product = share * lax.dot_general(
                values_t[j * nblocks + b],
                weights.astype(jnp.bfloat16),
                NN,
                preferred_element_type=jnp.float32,
            )
            found.append((one, total[:, :rows], product[:, :rows]))
            found.append((two, total[:, rows:], product[:, rows:]))
        for row, total, product in found:
            row_total[row] += total
            acc[row] += product
        return carry

    lax.fori_loop(0, steps, second_pass, 0)

    for j in range(heads_here):
        for a in range(nblocks):
            row = j * nblocks + a
            out[a, j] = (acc[row] * (1.0 / row_total[row])).T.astype(out.dtype)


def attend(tables, parcels, list_len):
    nblocks, parcel_rows, head_dim = parcels.shape
    heads_here = tables.shape[0] // PAIR_ROWS
    rows = parcel_rows // (heads_here * KINDS)
    factor = head_dim ** (-0.5) * math.log2(math.e)
    grid_rows = nblocks * heads_here
    slots = -(-heads_here * (list_len + 2 * nblocks) // (2 * GROUP)) * GROUP
    return pl.pallas_call(
        functools.partial(heads_kernel, factor),
        out_shape=jax.ShapeDtypeStruct((nblocks, heads_here, rows, head_dim), jnp.bfloat16),
        in_specs=[ANY, VMEM],
        out_specs=VMEM,
        scratch_shapes=[
            pltpu.VMEM((grid_rows, head_dim, rows), jnp.bfloat16),
            pltpu.VMEM((slots, rows, 2 * rows), jnp.float32),
            pltpu.VMEM((slots, 1, 2 * rows), jnp.float32),
            pltpu.SMEM(tables.shape, jnp.int32),
            pltpu.SemaphoreType.DMA,
            pltpu.VMEM((grid_rows, head_dim, rows), jnp.float32),
            pltpu.VMEM((grid_rows, 1, rows), jnp.float32),
            pltpu.VMEM((grid_rows, 1, rows), jnp.float32),
        ],
        compiler_params=pltpu.CompilerParams(vmem_limit_bytes=36 * 1024 * 1024),
        name="attend",
    )(tables, parcels)


def on_device(queries, key_vectors, value_vectors, keep_list, block_counts):
    peers = lax.axis_size("seq")
    me = lax.axis_index("seq").reshape(1)
    packed, order = pack(block_counts, queries, key_vectors, value_vectors, peers)
    parcels = lax.all_to_all(packed, "seq", split_axis=0, concat_axis=0, tiled=True)
    tables = own_tables(me, block_counts, order, keep_list, peers)
    attended = attend(tables, parcels, keep_list.shape[1])
    returned = lax.all_to_all(attended, "seq", split_axis=0, concat_axis=0, tiled=True)
    return unpack(order, returned)


def solution(mesh):
    tokens = P(("batch", "seq"), None)
    return jax.shard_map(
        on_device,
        mesh=mesh,
        in_specs=(tokens, tokens, tokens, tokens, P("batch")),
        out_specs=tokens,
        check_vma=False,
    )
```
